32 devices in a mesh: user: 16 (over z, y, x), isec: 2 (over core).
Axes of the slice: x: 2, y: 2, z: 4, core: 2. Of those that a mesh axis runs over, the one named last changes fastest.
Arguments:
- user_factors: float32 [8192, 512], P('user'), may hold values from -1.5 to 1.5
- item_factors: float32 [8192, 512], P(('user', 'isec')), may hold values from -1.5 to 1.5
- confidence: bfloat16 [16, 2, 4, 6, 128, 128], P('user', 'isec'), may hold values from 0.19921875 to 5
- tile_ids: int32 [16, 2, 4, 6], P('user', 'isec'), may hold values from 0 to 7, as said below
- tile_counts: int32 [16, 2, 4], P('user', 'isec'), may hold values from 1 to 6, as said below
Outputs:
- new_user_factors: float32 [8192, 512], P(('user', 'isec'))
- new_item_factors: float32 [8192, 512], P(('user', 'isec'))
The draws below stay inside these ranges and needn't reach their ends.
Inputs may be any that keep to these rules, and one draw needn't show every extreme that they name: `tile_ids`: the 6 positions of one list name different tiles. `tile_counts`: some list has all 6 positions live.
All inputs are finite; a program needn't handle non-finite values.
Results may differ from the reference program's by a relative error of at most 0.0003.
Values sent between devices are 32-bit elements; how exact they have to be, the bound alone decides.
No kernel may reach another device: no remote copies, remote signals or barrier semaphores. Data moves between devices by JAX's collectives and lax.ppermute only.
A program may use at most 64 MiB of HBM per device.

```python
import math
import jax
import jax.numpy as jnp
from jax import lax

RANK = 512
TILE = 128
USER_DEV = 512
ITEM_BLOCK = 256
TILES = 6
VISITS = 4
USERS = 8192
ITEMS = 8192
N_USER = 16
N_ISEC = 2


def draw_tile_ids(key, part):
    pair_count = USER_DEV // TILE * (ITEM_BLOCK // TILE)
    scores = jax.random.randint(key, (N_USER, N_ISEC, VISITS, pair_count), 0, 1 << 20) * pair_count + jnp.arange(pair_count, dtype=jnp.int32)
    ranking = jnp.argsort(scores, axis=-1, stable=True).astype(jnp.int32)
    return ranking[..., :TILES]


def draw_tile_counts(key, part):
    base_key, bias_key, spot_key = jax.random.split(jax.random.fold_in(key, 7), 3)
    base_counts = jax.random.randint(base_key, (N_USER, N_ISEC, VISITS), 1, TILES + 1)
    owner_bias = jax.random.randint(bias_key, (N_USER, 1, 1), -2, 3)
    counts_all = jnp.clip(base_counts + owner_bias, 1, TILES)
    total_lists = N_USER * N_ISEC * VISITS
    forced_spot = jax.random.randint(spot_key, (), 0, total_lists)
    flat_counts = counts_all.reshape(total_lists)
    flat_counts = jnp.where(jnp.arange(total_lists, dtype=jnp.int32) == forced_spot, TILES, flat_counts)
    return flat_counts.reshape(N_USER, N_ISEC, VISITS).astype(jnp.int32)


def block_scale(stream_key, extent, cuts, smallest, largest):
    factor_of = 1.0
    for axis_at, blocks in cuts:
        steps = jax.random.uniform(jax.random.fold_in(jax.random.fold_in(stream_key, 6), axis_at), (blocks,), jnp.float32, smallest / len(cuts), largest / len(cuts))
        factor_of = factor_of * jnp.repeat(jnp.exp(steps), extent[axis_at] // blocks).reshape((-1,) + (1,) * (len(extent) - 1 - axis_at))
    return factor_of


def normal_values(own_key, extent, spread, most, cuts=(), kind=jnp.bfloat16):
    drawn = jax.random.normal(own_key, extent, jnp.float32) * spread
    if len(cuts) > 0:
        drawn = block_scale(own_key, extent, cuts, -0.22, 0.18) * drawn
    return jnp.clip(drawn, min=-most, max=most).astype(kind)


def setup_inputs(seed: int = 0) -> dict:
    arg_keys = jax.random.split(jax.random.key(seed), 6)
    return {
        "user_factors": normal_values(arg_keys[0], (USERS, RANK), 0.25, 1.5, ((0, 16),), jnp.float32),
        "item_factors": normal_values(arg_keys[1], (ITEMS, RANK), 0.25, 1.5, ((0, 32),), jnp.float32),
        "confidence": jnp.clip(jnp.exp(math.log(5.0) - 3.2227897 * jax.random.uniform(arg_keys[2], (N_USER, N_ISEC, VISITS, TILES, TILE, TILE), jnp.float32) ** block_scale(arg_keys[2], (N_USER, N_ISEC, VISITS, TILES, TILE, TILE), ((0, 16), (1, 2)), -0.2, 0.2)), 0.19921875, 5.0).astype(jnp.bfloat16),
        "tile_ids": draw_tile_ids(jax.random.fold_in(arg_keys[5], 71), 0),
        "tile_counts": draw_tile_counts(jax.random.fold_in(arg_keys[5], 71), 0),
    }


item_rate = 0.02
user_rate = 0.005
shrinkage = 0.1


def visit_update(owner_tiles, item_tiles, weights, indices, limit):
    highest = lax.Precision.HIGHEST
    user_count = owner_tiles.shape[0]
    item_count = item_tiles.shape[0]
    tile_total = indices.shape[0]
    pick_user = (indices[:, None] // item_count == jnp.arange(user_count, dtype=jnp.int32)[None, :]).astype(jnp.float32)
    pick_item = (indices[:, None] % item_count == jnp.arange(item_count, dtype=jnp.int32)[None, :]).astype(jnp.float32)
    chosen_users = jnp.einsum("tu,uar->tar", pick_user, owner_tiles, precision=highest)
    chosen_items = jnp.einsum("tj,jbr->tbr", pick_item, item_tiles, precision=highest)
    predicted = jnp.einsum("tar,tbr->tab", chosen_users, chosen_items, precision=highest)
    live_mask = jnp.arange(tile_total, dtype=jnp.int32) < limit
    errors = jnp.where(live_mask[:, None, None], weights.astype(jnp.float32) * (predicted - 1.0), 0.0)
    item_grad = jnp.einsum("tab,tar->tbr", errors, chosen_users, precision=highest)
    item_step = jnp.einsum("tj,tbr->jbr", pick_item, item_grad, precision=highest)
    user_grad = jnp.einsum("tab,tbr->tar", errors, chosen_items, precision=highest)
    user_step = jnp.einsum("tu,tar->uar", pick_user, user_grad, precision=highest)
    new_items = item_tiles - item_rate * (item_step + shrinkage * item_tiles)
    return new_items, user_step


def reference(user_factors, item_factors, confidence, tile_ids, tile_counts):
    user_tile_count = USER_DEV // TILE
    item_tile_count = ITEM_BLOCK // TILE
    user_tiles = user_factors.reshape(N_USER, user_tile_count, TILE, RANK)
    blocks = item_factors.reshape(N_USER, N_ISEC, item_tile_count, TILE, RANK)
    user_total = jnp.zeros((N_USER, user_tile_count, TILE, RANK), jnp.float32)

    def one_owner(packed):
        owner_tiles, owner_blocks, owner_weights, owner_ids, owner_counts = packed
        section_update = jax.vmap(visit_update, in_axes=(None, 0, 0, 0, 0))
        new_blocks, steps = section_update(owner_tiles, owner_blocks, owner_weights, owner_ids, owner_counts)
        return new_blocks, jnp.sum(steps, axis=0)

    for visit in range(VISITS):
        current = jnp.roll(blocks, visit, axis=0)
        new_blocks, steps = lax.map(one_owner, (user_tiles, current, confidence[:, :, visit], tile_ids[:, :, visit], tile_counts[:, :, visit]))
        blocks = jnp.roll(new_blocks, -visit, axis=0)
        user_total = user_total + steps
    gradient = user_total.reshape(USERS, RANK)
    new_users = user_factors - user_rate * (gradient + shrinkage * user_factors)
    return new_users, blocks.reshape(ITEMS, RANK)
```

```python
import functools

import jax
import jax.numpy as jnp
from jax import lax
from jax.experimental import pallas as pl
from jax.experimental.pallas import tpu as pltpu
from jax.sharding import PartitionSpec as P

TILE = 128

item_rate = 0.02
user_rate = 0.005
shrinkage = 0.1

MIB = 1 << 20


def shifted(block, axis, distance):
    count = lax.axis_size(axis)
    return lax.ppermute(block, axis, [((i - distance) % count, i) for i in range(count)])


def halves(x):
    high = x.astype(jnp.bfloat16)
    return high, (x - high.astype(jnp.float32)).astype(jnp.bfloat16)


def product(a, b, dims):
    dot = functools.partial(
        lax.dot_general, dimension_numbers=(dims, ((), ())), preferred_element_type=jnp.float32
    )
    return dot(a[0], b[0]) + (dot(a[0], b[1]) + dot(a[1], b[0]))


def visit_kernel(visit, tile, item_count, ids, counts, users, items, weights, new_items, errors, dense):
    dense[...] = jnp.zeros_like(dense)
    for n in range(weights.shape[0]):
        k = ids[visit, n]

        @pl.when((n < counts[visit]) & (k % item_count == tile))
        def _():
            rows = pl.ds(pl.multiple_of(k // item_count * TILE, TILE), TILE)
            dense[rows, :] = weights[n].astype(jnp.float32)

    p = halves(users[...])
    q = items[...]
    predicted = product(p, halves(q), ((1,), (1,)))
    error = dense[...] * (predicted - 1.0)
    errors[...] = error
    step = product(halves(error.T), p, ((1,), (0,)))
    new_items[...] = q - item_rate * (step + shrinkage * q)


def visit_call(visit, tile, item_count, users, items, weights, ids, counts):
    user_rows, rank = users.shape
    block = weights.shape[1:]
    flops = 2 * 3 * 2 * user_rows * rank * TILE
    return pl.pallas_call(
        functools.partial(visit_kernel, visit, tile, item_count),
        grid=(1,),
        out_shape=(
            jax.ShapeDtypeStruct(items.shape, jnp.float32),
            jax.ShapeDtypeStruct((user_rows, TILE), jnp.float32),
        ),
        in_specs=[
            pl.BlockSpec(memory_space=pltpu.SMEM),
            pl.BlockSpec(memory_space=pltpu.SMEM),
            pl.BlockSpec(users.shape, lambda i: (0, 0)),
            pl.BlockSpec(items.shape, lambda i: (0, 0)),
            pl.BlockSpec((None, *block), lambda i: (visit, 0, 0, 0)),
        ],
        out_specs=(
            pl.BlockSpec(items.shape, lambda i: (0, 0)),
            pl.BlockSpec((user_rows, TILE), lambda i: (0, 0)),
        ),
        scratch_shapes=[pltpu.VMEM((user_rows, TILE), jnp.float32)],
        cost_estimate=pl.CostEstimate(flops=flops, bytes_accessed=2 * MIB, transcendentals=0),
        compiler_params=pltpu.CompilerParams(vmem_limit_bytes=32 * MIB),
        name="visit_update",
    )(ids, counts, users, items, weights)


def gradient_kernel(pairs, *refs):
    total = refs[-1]
    for i in range(pairs):
        term = product(halves(refs[i][...]), halves(refs[pairs + i][...]), ((1,), (0,)))
        total[...] = term if i == 0 else total[...] + term


def gradient_call(errors, items):
    shape = (errors[0].shape[0], items[0].shape[1])
    pairs = len(errors)
    return pl.pallas_call(
        functools.partial(gradient_kernel, pairs),
        out_shape=jax.ShapeDtypeStruct(shape, jnp.float32),
        in_specs=[pl.BlockSpec(memory_space=pltpu.VMEM)] * (2 * pairs),
        out_specs=pl.BlockSpec(memory_space=pltpu.VMEM),
        cost_estimate=pl.CostEstimate(
            flops=2 * 3 * pairs * TILE * shape[0] * shape[1], bytes_accessed=5 * MIB, transcendentals=0
        ),
        compiler_params=pltpu.CompilerParams(vmem_limit_bytes=32 * MIB),
        name="user_gradient",
    )(*errors, *items)


def on_device(user_factors, item_factors, confidence, tile_ids, tile_counts):
    visits = confidence.shape[2]
    item_count = item_factors.shape[0] // TILE
    weights, ids, counts = confidence[0, 0], tile_ids[0, 0], tile_counts[0, 0]
    chunks = [item_factors[j * TILE : (j + 1) * TILE] for j in range(item_count)]
    errors, used = [], []
    for visit in range(visits):
        for j in range(item_count):
            if visit > 0:
                chunks[j] = shifted(chunks[j], "user", 1)
            used.append(chunks[j])
            chunks[j], error = visit_call(
                visit, j, item_count, user_factors, chunks[j], weights, ids, counts
            )
            errors.append(error)
    chunks = [shifted(chunk, "user", 1 - visits) for chunk in chunks]
    gradient = gradient_call(errors, used)
    sections, me = lax.axis_size("isec"), lax.axis_index("isec")
    share = user_factors.shape[0] // sections

    def part(array, section):
        return lax.dynamic_slice_in_dim(array, section * share, share, 0)

    summed = part(gradient, me)
    for away in range(1, sections):
        summed = summed + shifted(part(gradient, (me + away) % sections), "isec", away)
    own = part(user_factors, me)
    return own - user_rate * (summed + shrinkage * own), jnp.concatenate(chunks, axis=0)


def solution(mesh):
    return jax.shard_map(
        on_device,
        mesh=mesh,
        in_specs=(
            P("user", None),
            P(("user", "isec"), None),
            P("user", "isec", None, None, None, None),
            P("user", "isec", None, None),
            P("user", "isec", None),
        ),
        out_specs=(P(("user", "isec"), None), P(("user", "isec"), None)),
        check_vma=False,
    )
```

```python
import functools

import jax
import jax.numpy as jnp
from jax import lax
from jax.experimental import pallas as pl
from jax.experimental.pallas import tpu as pltpu
from jax.sharding import PartitionSpec as P

TILE = 128
ROWS = 128

item_rate = 0.02
user_rate = 0.005
shrinkage = 0.1

MIB = 1 << 20
FIRST_LIMIT = 63 * MIB
LIMIT = 16 * MIB
SMEM, HBM, VMEM = (pl.BlockSpec(memory_space=s) for s in (pltpu.SMEM, pltpu.HBM, pltpu.VMEM))


def shifted(block, axis, distance):
    count = lax.axis_size(axis)
    return lax.ppermute(block, axis, [((i - distance) % count, i) for i in range(count)])


def f32(*shape):
    return jax.ShapeDtypeStruct(shape, jnp.float32)


def halves(x):
    high = x.astype(jnp.bfloat16)
    return high, (x - high.astype(jnp.float32)).astype(jnp.bfloat16)


def dot(a, b, left, right):
    dims = (((left,), (right,)), ((), ()))
    return lax.dot_general(a, b, dims, preferred_element_type=jnp.float32)


def product(a, b, right):
    count = a[0].shape[0]
    both = dot(jnp.concatenate(a, axis=0), b[0], 1, right)
    return both[:count] + (both[count:] + dot(a[0], b[1], 1, right))


def errors_of(q, p, weights):
    return weights * (product(halves(q), p, 1) - 1.0)


def stepped(q, error, p):
    return q - item_rate * (product(halves(error), p, 0) + shrinkage * q)


def gradient(error, q):
    e, r = halves(error), halves(q)
    both = dot(jnp.concatenate(e, axis=0), jnp.concatenate([r[0], r[0]], axis=0), 0, 0)
    return both + dot(e[0], r[1], 0, 0)


def fill(dense, lists, ids, counts, visit, first, item_count):
    dense[...] = jnp.zeros_like(dense)
    rows = dense.shape[0]
    for n in range(lists.shape[0]):
        k = ids[visit, n]
        row = (k % item_count - first) * TILE

        @pl.when((n < counts[visit]) & (row >= 0) & (row < rows))
        def _():
            place = (
                pl.ds(pl.multiple_of(row, TILE), TILE),
                pl.ds(pl.multiple_of(k // item_count * TILE, TILE), TILE),
            )
            dense[place] = lists[n].astype(jnp.float32).T.astype(dense.dtype)


def first_kernel(tile, item_count, place, ids, counts, users, items, weights, *refs):
    del place
    *chunks, p_rows, q_rows, lists, dense, own_ids, own_counts, arrived = refs
    copies = [
        pltpu.make_async_copy(source, target, arrived.at[i])
        for i, (source, target) in enumerate(
            (
                (ids, own_ids),
                (counts, own_counts),
                (weights.at[0], lists),
                (items.at[pl.ds(tile * TILE, TILE)], q_rows),
                (users, p_rows),
            )
        )
    ]
    for copy in copies:
        copy.start()
    for copy in copies[:3]:
        copy.wait()
    fill(dense, lists, own_ids, own_counts, 0, tile, item_count)
    for copy in copies[3:]:
        copy.wait()
    q, p = q_rows[...], halves(p_rows[...])
    after = stepped(q, errors_of(q, p, dense[...]), p)
    for c, chunk in enumerate(chunks):
        chunk[...] = after[c * ROWS : (c + 1) * ROWS]


def split_kernel(users, high, low):
    high[...], low[...] = halves(users[...])


def dense_kernel(visit, item_count, ids, counts, weights, *refs):
    fill(refs[-1], weights.at[visit], ids, counts, visit, 0, item_count)


def visit_kernel(first, kept, high, low, dense, items, *refs):
    new_items, errors, used = refs[-3:]
    q, p = items[...], (high[...], low[...])
    rows = pl.ds(first, q.shape[0])
    e = errors_of(q, p, dense[rows, :].astype(jnp.float32))
    new_items[...] = stepped(q, e, p)
    rows = pl.ds(kept, q.shape[0])
    errors[rows, :] = e
    used[rows, :] = q


def early_kernel(item_count, block_rows, ids, counts, weights, high, low, items, errors, used, total, dense):
    fill(dense, weights.at[0], ids, counts, 0, 0, item_count)
    q = items[...]
    e = errors_of(q, (high[...], low[...]), dense[...].astype(jnp.float32))
    total[...] = gradient(e, q) + gradient(errors[:block_rows, :], used[:block_rows, :])


def gradient_kernel(first, shares, place, errors, used, total, new_total, *parts):
    new_total[...] = total[...] + gradient(errors[first:, :], used[first:, :])
    share = total.shape[0] // shares
    for away, part in enumerate(parts, 1):
        start = lax.rem(place[0] + away, shares) * share
        part[...] = new_total[pl.ds(pl.multiple_of(start, share), share), :]


def users_kernel(place, users, total, *refs):
    *received, new_items, new_users, same_items = refs
    del new_items, same_items
    share = new_users.shape[0]
    rows = pl.ds(pl.multiple_of(place[0] * share, share), share)
    summed = total[rows, :]
    for term in received:
        summed = summed + term[...]
    p = users[rows, :]
    new_users[...] = p - user_rate * (summed + shrinkage * p)


def place_kernel(first, chunk, *refs):
    whole, moved = refs[-2:]
    store = pltpu.make_async_copy(chunk, whole.at[pl.ds(first, chunk.shape[0])], moved)
    store.start()
    store.wait()


def call(kernel, name, out_shape, in_specs, args, flops=0, limit=LIMIT, **more):
    cost = pl.CostEstimate(flops=flops, bytes_accessed=MIB, transcendentals=0)
    return pl.pallas_call(
        kernel,
        name=name,
        out_shape=out_shape,
        in_specs=in_specs,
        cost_estimate=cost,
        compiler_params=pltpu.CompilerParams(vmem_limit_bytes=limit),
        **more,
    )(*args)


def on_device(user_factors, item_factors, confidence, tile_ids, tile_counts):
    visits = confidence.shape[2]
    user_rows, rank = user_factors.shape
    block_rows = item_factors.shape[0]
    item_count = block_rows // TILE
    sections = lax.axis_size("isec")
    place = lax.axis_index("isec").astype(jnp.int32).reshape(1)
    weights, ids, counts = confidence[0, 0], tile_ids[0, 0], tile_counts[0, 0]
    unit = 2 * 3 * user_rows * rank * ROWS
    wait = 8 << 30

    chunks = []
    for j in range(item_count):
        chunks += call(
            functools.partial(first_kernel, j, item_count),
            "first_visit",
            (f32(ROWS, rank),) * (TILE // ROWS),
            [HBM] * 6,
            (place, ids, counts, user_factors, item_factors, weights),
            flops=2 * unit * TILE // ROWS,
            limit=FIRST_LIMIT,
            scratch_shapes=[
                pltpu.VMEM((user_rows, rank), jnp.float32),
                pltpu.VMEM((TILE, rank), jnp.float32),
                pltpu.VMEM(weights.shape[1:], weights.dtype),
                pltpu.VMEM((TILE, user_rows), jnp.float32),
                pltpu.SMEM(ids.shape, jnp.int32),
                pltpu.SMEM(counts.shape, jnp.int32),
                pltpu.SemaphoreType.DMA((5,)),
            ],
        )
    half = jax.ShapeDtypeStruct((user_rows, rank), jnp.bfloat16)
    split = call(
        split_kernel, "split_users", (half, half), [VMEM], (user_factors,), out_specs=(VMEM,) * 2
    )
    tiles = jax.ShapeDtypeStruct((block_rows, user_rows), weights.dtype)
    lists = (ids, counts, weights)
    kept_rows = (visits - 1) * block_rows
    kept, total = (), ()
    for visit in range(1, visits):
        dense = call(
            functools.partial(dense_kernel, visit, item_count),
            "dense_tiles",
            tiles,
            [SMEM, SMEM] + [VMEM] * (1 + len(kept)),
            (*lists, *kept),
            out_specs=VMEM,
        )
        for c in range(len(chunks)):
            if visit == visits - 1 and c == len(chunks) - 1:
                total = (
                    call(
                        functools.partial(early_kernel, item_count, block_rows),
                        "early_gradient",
                        f32(user_rows, rank),
                        [SMEM, SMEM] + [VMEM] * 6,
                        (*lists, *split, item_factors, *kept),
                        flops=3 * unit * len(chunks),
                        out_specs=VMEM,
                        scratch_shapes=[pltpu.VMEM(tiles.shape, tiles.dtype)],
                    ),
                )
            first = (visit - 1) * block_rows + c * ROWS
            chunks[c], *kept = call(
                functools.partial(visit_kernel, c * ROWS, first),
                "visit_update",
                (f32(ROWS, rank), f32(kept_rows, user_rows), f32(kept_rows, rank)),
                [VMEM] * (4 + len(kept) + len(total)),
                (*split, dense, shifted(chunks[c], "user", 1), *kept, *total),
                flops=2 * unit,
                out_specs=(VMEM,) * 3,
                input_output_aliases={4: 1, 5: 2} if kept else {},
            )
    away = sections - 1
    total, *parts = call(
        functools.partial(gradient_kernel, block_rows, sections),
        "user_gradient",
        (f32(user_rows, rank),) + (f32(user_rows // sections, rank),) * away,
        [SMEM] + [VMEM] * 3,
        (place, *kept, *total),
        flops=2 * unit * len(chunks),
        out_specs=(VMEM,) * (1 + away),
        input_output_aliases={3: 0},
    )

    chunks = [shifted(chunk, "user", 1 - visits) for chunk in chunks]
    received = [shifted(part, "isec", away) for away, part in enumerate(parts, 1)]
    new_items = ()
    for c, chunk in enumerate(chunks):
        new_items = (
            call(
                functools.partial(place_kernel, c * ROWS),
                "place_items",
                f32(block_rows, rank),
                [VMEM] + [HBM] * len(new_items),
                (chunk, *new_items),
                flops=wait,
                limit=4 * MIB,
                out_specs=HBM,
                scratch_shapes=[pltpu.SemaphoreType.DMA],
                input_output_aliases={1: 0} if new_items else {},
            ),
        )
    return call(
        users_kernel,
        "new_users",
        (f32(user_rows // sections, rank), f32(block_rows, rank)),
        [SMEM, VMEM, VMEM] + [VMEM] * len(received) + [HBM],
        (place, user_factors, total, *received, *new_items),
        flops=wait,
        out_specs=(VMEM, HBM),
        input_output_aliases={3 + len(received): 1},
    )


def solution(mesh):
    return jax.shard_map(
        on_device,
        mesh=mesh,
        in_specs=(
            P("user", None),
            P(("user", "isec"), None),
            P("user", "isec", None, None, None, None),
            P("user", "isec", None, None),
            P("user", "isec", None),
        ),
        out_specs=(P(("user", "isec"), None), P(("user", "isec"), None)),
        check_vma=False,
    )
```

```python
import functools

import jax
import jax.numpy as jnp
from jax import lax
from jax.experimental import pallas as pl
from jax.experimental.pallas import tpu as pltpu
from jax.sharding import PartitionSpec as P

TILE = 128
SIZES = (64, 64, 64, 64)
GROUPS = ((0, 1), (2,), (3,))
EARLY = 1

item_rate = 0.02
user_rate = 0.005
shrinkage = 0.1

MIB = 1 << 20
LIMIT = 16 * MIB
SMEM, HBM, VMEM = (pl.BlockSpec(memory_space=s) for s in (pltpu.SMEM, pltpu.HBM, pltpu.VMEM))


def shifted(block, axis, distance):
    count = lax.axis_size(axis)
    return lax.ppermute(block, axis, [((i - distance) % count, i) for i in range(count)])


def f32(*shape):
    return jax.ShapeDtypeStruct(shape, jnp.float32)


def halves(x):
    high = x.astype(jnp.bfloat16)
    return high, (x - high.astype(jnp.float32)).astype(jnp.bfloat16)


def dot(a, b, left, right):
    dims = (((left,), (right,)), ((), ()))
    return lax.dot_general(a, b, dims, preferred_element_type=jnp.float32)


def product(a, b, right):
    count = a[0].shape[0]
    both = dot(jnp.concatenate(a, axis=0), b[0], 1, right)
    return both[:count] + (both[count:] + dot(a[0], b[1], 1, right))


def errors_of(q, p, weights):
    return weights * (product(halves(q), p, 1) - 1.0)


def stepped(q, error, p):
    return q - item_rate * (product(halves(error), p, 0) + shrinkage * q)


def gradient(error, q):
    e, r = halves(error), halves(q)
    both = dot(jnp.concatenate(e, axis=0), jnp.concatenate([r[0], r[0]], axis=0), 0, 0)
    return both + dot(e[0], r[1], 0, 0)


def fill(dense, lists, ids, counts, visit, first, item_count):
    dense[...] = jnp.zeros_like(dense)
    rows = dense.shape[0]
    for n in range(lists.shape[0]):
        k = ids[visit, n]
        row = (k % item_count - first) * TILE

        @pl.when((n < counts[visit]) & (row >= 0) & (row < rows))
        def _():
            place = (
                pl.ds(pl.multiple_of(row, TILE), TILE),
                pl.ds(pl.multiple_of(k // item_count * TILE, TILE), TILE),
            )
            dense[place] = lists[n].astype(jnp.float32).T.astype(dense.dtype)


def first_kernel(item_count, place, ids, counts, users, items, weights, *refs):
    del place
    new_items, errors, used, high, low, p_rows, rest, lists, *refs = refs
    q_rows, first_lists, dense, own_ids, own_counts, arrived = refs
    pairs = [
        (ids, own_ids),
        (counts, own_counts),
        (weights.at[0], first_lists),
        (items.at[pl.ds(0, q_rows.shape[0])], q_rows),
        (users, p_rows),
        (weights, lists),
    ]
    pairs.append((items.at[pl.ds(q_rows.shape[0], rest.shape[0])], rest))
    copies = [pltpu.make_async_copy(*pair, arrived.at[i]) for i, pair in enumerate(pairs)]
    for copy in copies:
        copy.start()
    for copy in copies[:3]:
        copy.wait()
    fill(dense, first_lists, own_ids, own_counts, 0, 0, item_count)
    copies[3].wait()
    q = q_rows[...]
    copies[4].wait()
    p = halves(p_rows[...])
    high[...], low[...] = p
    e = errors_of(q, p, dense[pl.ds(0, q.shape[0]), :])
    new_items[...] = stepped(q, e, p)
    errors[pl.ds(0, q.shape[0]), :] = e
    used[pl.ds(0, q.shape[0]), :] = q
    for copy in copies[5:]:
        copy.wait()


def dense_kernel(wanted, item_count, ids, counts, weights, *refs):
    for visit, target in zip(wanted, refs[-len(wanted) :], strict=True):
        fill(target, weights.at[visit], ids, counts, visit, 0, item_count)


def visit_kernel(first, count, source, kept, joined, high, low, dense, items, *refs):
    new_items, errors, used = refs[-3:]
    start = 0
    for chunk in refs[len(refs) - 3 - joined : -3]:
        new_items[pl.ds(start, chunk.shape[0]), :] = chunk[...]
        start += chunk.shape[0]
    q, p = items[pl.ds(source, count), :], (high[...], low[...])
    e = errors_of(q, p, dense[pl.ds(first, count), :].astype(jnp.float32))
    new_items[pl.ds(start, count), :] = stepped(q, e, p)
    rows = pl.ds(kept, count)
    errors[rows, :] = e
    used[rows, :] = q


def early_kernel(split, errors, used, total):
    total[...] = gradient(errors[:split, :], used[:split, :])


def gradient_kernel(split, shares, place, errors, used, total, new_total, *parts):
    new_total[...] = total[...] + gradient(errors[split:, :], used[split:, :])
    share = total.shape[0] // shares
    for away, part in enumerate(parts, 1):
        start = lax.rem(place[0] + away, shares) * share
        part[...] = new_total[pl.ds(pl.multiple_of(start, share), share), :]


def users_kernel(place, users, total, *refs):
    *received, new_items, new_users, same_items = refs
    del new_items, same_items
    share = new_users.shape[0]
    rows = pl.ds(pl.multiple_of(place[0] * share, share), share)
    summed = total[rows, :]
    for term in received:
        summed = summed + term[...]
    p = users[rows, :]
    new_users[...] = p - user_rate * (summed + shrinkage * p)


def place_kernel(starts, *refs):
    *chunks, whole, moved = refs
    stores = [
        pltpu.make_async_copy(chunk, whole.at[pl.ds(start, chunk.shape[0])], moved.at[i])
        for i, (start, chunk) in enumerate(zip(starts, chunks, strict=True))
    ]
    for store in stores:
        store.start()
    for store in stores:
        store.wait()


def call(kernel, name, out_shape, in_specs, args, flops=0, limit=LIMIT, **more):
    cost = pl.CostEstimate(flops=flops, bytes_accessed=MIB, transcendentals=0)
    return pl.pallas_call(
        kernel,
        name=name,
        out_shape=out_shape,
        in_specs=in_specs,
        cost_estimate=cost,
        compiler_params=pltpu.CompilerParams(vmem_limit_bytes=limit),
        **more,
    )(*args)


def on_device(user_factors, item_factors, confidence, tile_ids, tile_counts):
    visits = confidence.shape[2]
    user_rows, rank = user_factors.shape
    block_rows = item_factors.shape[0]
    item_count = block_rows // TILE
    sections = lax.axis_size("isec")
    place = lax.axis_index("isec").astype(jnp.int32).reshape(1)
    weights, ids, counts = confidence[0, 0], tile_ids[0, 0], tile_counts[0, 0]
    unit = 2 * 3 * user_rows * rank
    wait = 8 << 30

    def vmem(shape, dtype=jnp.float32):
        return pltpu.VMEM(shape, dtype)

    def in_hbm(*arrays):
        return tuple(pltpu.with_memory_space_constraint(array, pltpu.HBM) for array in arrays)

    sizes = SIZES if sum(SIZES) == block_rows else (TILE,) * item_count
    starts = [sum(sizes[:i]) for i in range(len(sizes))]
    kept_shape = (visits * block_rows, rank), (visits * block_rows, user_rows)
    chunk, errors, used, *ready, users, rest, lists = call(
        functools.partial(first_kernel, item_count),
        "first_visit",
        (
            vmem((sizes[0], rank)),
            vmem(kept_shape[1]),
            vmem(kept_shape[0]),
            vmem((user_rows, rank), jnp.bfloat16),
            vmem((user_rows, rank), jnp.bfloat16),
            vmem((user_rows, rank)),
            vmem((block_rows - sizes[0], rank)),
            vmem(weights.shape, weights.dtype),
        ),
        [HBM] * 6,
        in_hbm(place, ids, counts, user_factors, item_factors, weights),
        flops=2 * unit * sizes[0],
        out_specs=(VMEM,) * 8,
        scratch_shapes=[
            pltpu.VMEM((sizes[0], rank), jnp.float32),
            pltpu.VMEM(weights.shape[1:], weights.dtype),
            pltpu.VMEM((TILE, user_rows), jnp.float32),
            pltpu.SMEM(ids.shape, jnp.int32),
            pltpu.SMEM(counts.shape, jnp.int32),
            pltpu.SemaphoreType.DMA((7,)),
        ],
    )
    kept = (errors, used)

    def dense_call(wanted, after):
        return call(
            functools.partial(dense_kernel, wanted, item_count),
            "dense_tiles",
            (jax.ShapeDtypeStruct((block_rows, user_rows), weights.dtype),) * len(wanted),
            [SMEM, SMEM] + [VMEM] * (1 + len(after)),
            (ids, counts, lists, *after),
            out_specs=(VMEM,) * len(wanted),
        )

    def visit_call(visit, c, dense, items, source, kept, after=(), joined=()):
        start, size = starts[c], sizes[c]
        return call(
            functools.partial(visit_kernel, start, size, source, visit * block_rows + start, len(joined)),
            "visit_update",
            (
                f32(size + sum(chunk.shape[0] for chunk in joined), rank),
                f32(*kept_shape[1]),
                f32(*kept_shape[0]),
            ),
            [VMEM] * (6 + len(after) + len(joined)),
            (*ready, dense, items, *kept, *after, *joined),
            flops=2 * unit * size,
            out_specs=(VMEM,) * 3,
            input_output_aliases={4: 1, 5: 2},
        )

    groups = GROUPS if len(sizes) == GROUPS[-1][-1] + 1 else [(c,) for c in range(len(sizes))]
    chunks, returned = [chunk], []
    opening, dense = dense_call((0, 1), ())
    for c in range(1, len(sizes)):
        chunk, *kept = visit_call(0, c, opening, rest, starts[c] - sizes[0], kept)
        chunks.append(chunk)
    split = visits // 2 * block_rows
    for visit in range(1, visits):
        if visit > 1:
            (dense,) = dense_call((visit,), kept)
        for c in range(len(sizes)):
            last = visit == visits - 1
            after = ()
            if last and c == min(EARLY, len(sizes) - 1):
                total = call(
                    functools.partial(early_kernel, split),
                    "early_gradient",
                    f32(user_rows, rank),
                    [VMEM] * 2,
                    kept,
                    flops=unit * split,
                    out_specs=VMEM,
                )
                after = (total,)
            group = next(group for group in groups if c in group)
            joined = [chunks[i] for i in group[:-1]] if last and c == group[-1] else ()
            chunks[c], *kept = visit_call(
                visit, c, dense, shifted(chunks[c], "user", 1), 0, kept, after, joined
            )
            if last and c == group[-1]:
                returned.append(shifted(chunks[c], "user", 1 - visits))
    away = sections - 1
    total, *parts = call(
        functools.partial(gradient_kernel, split, sections),
        "user_gradient",
        (f32(user_rows, rank),) + (f32(user_rows // sections, rank),) * away,
        [SMEM] + [VMEM] * 3,
        (place, *kept, total),
        flops=unit * (visits * block_rows - split),
        out_specs=(VMEM,) * (1 + away),
        input_output_aliases={3: 0},
    )

    received = [shifted(part, "isec", away) for away, part in enumerate(parts, 1)]
    new_items = call(
        functools.partial(place_kernel, [starts[group[0]] for group in groups]),
        "place_items",
        f32(block_rows, rank),
        [VMEM] * len(returned),
        returned,
        flops=wait,
        limit=4 * MIB,
        out_specs=HBM,
        scratch_shapes=[pltpu.SemaphoreType.DMA((len(returned),))],
    )
    return call(
        users_kernel,
        "new_users",
        (f32(user_rows // sections, rank), f32(block_rows, rank)),
        [SMEM, VMEM, VMEM] + [VMEM] * len(received) + [HBM],
        (place, users, total, *received, new_items),
        flops=wait,
        out_specs=(VMEM, HBM),
        input_output_aliases={3 + len(received): 1},
    )


def solution(mesh):
    return jax.shard_map(
        on_device,
        mesh=mesh,
        in_specs=(
            P("user", None),
            P(("user", "isec"), None),
            P("user", "isec", None, None, None, None),
            P("user", "isec", None, None),
            P("user", "isec", None),
        ),
        out_specs=(P(("user", "isec"), None), P(("user", "isec"), None)),
        check_vma=False,
    )
```

```python
import functools

import jax
import jax.numpy as jnp
from jax import lax
from jax.experimental import pallas as pl
from jax.experimental.pallas import tpu as pltpu
from jax.sharding import PartitionSpec as P

TILE = 128
FIRST_BACK = 0
PIECES = 4

item_rate = 0.02
user_rate = 0.005
shrinkage = 0.1

MIB = 1 << 20
LIMIT = 16 * MIB
SMEM, HBM, VMEM = (pl.BlockSpec(memory_space=s) for s in (pltpu.SMEM, pltpu.HBM, pltpu.VMEM))


def shifted(block, axis, distance):
    count = lax.axis_size(axis)
    return lax.ppermute(block, axis, [((i - distance) % count, i) for i in range(count)])


def f32(*shape):
    return jax.ShapeDtypeStruct(shape, jnp.float32)


def halves(x):
    high = x.astype(jnp.bfloat16)
    return high, (x - high.astype(jnp.float32)).astype(jnp.bfloat16)


def dot(a, b, left, right):
    dims = (((left,), (right,)), ((), ()))
    return lax.dot_general(a, b, dims, preferred_element_type=jnp.float32)


def product(a, b, right):
    count = a[0].shape[0]
    both = dot(jnp.concatenate(a, axis=0), b[0], 1, right)
    return both[:count] + (both[count:] + dot(a[0], b[1], 1, right))


def errors_of(q, p, weights):
    return weights * (product(halves(q), p, 1) - 1.0)


def stepped(q, error, p):
    return q - item_rate * (product(halves(error), p, 0) + shrinkage * q)


def gradient(error, q):
    e, r = halves(error), halves(q)
    both = dot(jnp.concatenate(e, axis=0), jnp.concatenate([r[0], r[0]], axis=0), 0, 0)
    return both + dot(e[0], r[1], 0, 0)


def fill(dense, lists, ids, counts, visit, first, item_count):
    dense[...] = jnp.zeros_like(dense)
    rows = dense.shape[0]
    for n in range(lists.shape[0]):
        k = ids[visit, n]
        row = (k % item_count - first) * TILE

        @pl.when((n < counts[visit]) & (row >= 0) & (row < rows))
        def _():
            place = (
                pl.ds(pl.multiple_of(row, TILE), TILE),
                pl.ds(pl.multiple_of(k // item_count * TILE, TILE), TILE),
            )
            dense[place] = lists[n].astype(jnp.float32).T.astype(dense.dtype)


def first_kernel(item_count, ids, counts, users, items, weights, *refs):
    new_items, errors, used, high, low, p_rows, rest, lists, *refs = refs
    q_rows, first_lists, dense, own_ids, own_counts, arrived = refs
    pairs = [
        (ids, own_ids),
        (counts, own_counts),
        (weights.at[0], first_lists),
        (items.at[pl.ds(0, q_rows.shape[0])], q_rows),
        (users, p_rows),
        (weights, lists),
    ]
    pairs.append((items.at[pl.ds(q_rows.shape[0], rest.shape[0])], rest))
    copies = [pltpu.make_async_copy(*pair, arrived.at[i]) for i, pair in enumerate(pairs)]
    for copy in copies:
        copy.start()
    for copy in copies[:3]:
        copy.wait()
    fill(dense, first_lists, own_ids, own_counts, 0, 0, item_count)
    copies[3].wait()
    q = q_rows[...]
    copies[4].wait()
    p = halves(p_rows[...])
    high[...], low[...] = p
    e = errors_of(q, p, dense[pl.ds(0, q.shape[0]), :])
    new_items[...] = stepped(q, e, p)
    errors[pl.ds(0, q.shape[0]), :] = e
    used[pl.ds(0, q.shape[0]), :] = q
    for copy in copies[5:]:
        copy.wait()


def dense_kernel(wanted, item_count, ids, counts, weights, *refs):
    for visit, target in zip(wanted, refs[-len(wanted) :], strict=True):
        fill(target, weights.at[visit], ids, counts, visit, 0, item_count)


def visit_kernel(first, source, kept, joined, pieces, high, low, dense, items, *refs):
    *outputs, errors, used = refs[len(refs) - 2 - pieces :]
    q, p = items[pl.ds(source, TILE), :], (high[...], low[...])
    e = errors_of(q, p, dense[pl.ds(first, TILE), :].astype(jnp.float32))
    after = stepped(q, e, p)
    start = 0
    if joined:
        rows = refs[len(refs) - 3 - pieces]
        outputs[0][pl.ds(0, joined), :] = rows[...]
        outputs[0][pl.ds(joined, TILE), :] = after
    else:
        for output in outputs:
            output[...] = after[start : start + output.shape[0]]
            start += output.shape[0]
    rows = pl.ds(kept, TILE)
    errors[rows, :] = e
    used[rows, :] = q


def early_kernel(split, errors, used, total):
    total[...] = gradient(errors[:split, :], used[:split, :])


def gradient_kernel(split, shares, errors, used, total, new_total, *parts):
    new_total[...] = total[...] + gradient(errors[split:, :], used[split:, :])
    share = total.shape[0] // shares
    for i, part in enumerate(parts):
        away, piece = i // PIECES + 1, i % PIECES
        size = part.shape[0]
        start = lax.rem(lax.axis_index("isec") + away, shares) * share + piece * size
        part[...] = new_total[pl.ds(pl.multiple_of(start, size), size), :]


def users_kernel(users, total, *refs):
    *received, new_users = refs
    share = new_users.shape[0]
    size = share // PIECES
    for piece in range(PIECES):
        start = lax.axis_index("isec") * share + piece * size
        rows = pl.ds(pl.multiple_of(start, size), size)
        summed = total[rows, :]
        for term in received[piece::PIECES]:
            summed = summed + term[...]
        p = users[rows, :]
        new_users[pl.ds(piece * size, size), :] = p - user_rate * (summed + shrinkage * p)


def place_kernel(*refs):
    *chunks, whole, moved = refs
    start, stores = 0, []
    for i, chunk in enumerate(chunks):
        target = whole.at[pl.ds(start, chunk.shape[0])]
        stores.append(pltpu.make_async_copy(chunk, target, moved.at[i]))
        start += chunk.shape[0]
    for store in stores:
        store.start()
    for store in stores:
        store.wait()


def call(kernel, name, out_shape, in_specs, args, flops=0, limit=LIMIT, **more):
    cost = pl.CostEstimate(flops=flops, bytes_accessed=MIB, transcendentals=0)
    return pl.pallas_call(
        kernel,
        name=name,
        out_shape=out_shape,
        in_specs=in_specs,
        cost_estimate=cost,
        compiler_params=pltpu.CompilerParams(vmem_limit_bytes=limit),
        **more,
    )(*args)


def on_device(user_factors, item_factors, confidence, tile_ids, tile_counts):
    visits = confidence.shape[2]
    user_rows, rank = user_factors.shape
    block_rows = item_factors.shape[0]
    item_count = block_rows // TILE
    sections = lax.axis_size("isec")
    weights, ids, counts = confidence[0, 0], tile_ids[0, 0], tile_counts[0, 0]
    unit = 2 * 3 * user_rows * rank

    def vmem(shape, dtype=jnp.float32):
        return pltpu.VMEM(shape, dtype)

    def in_hbm(*arrays):
        return tuple(pltpu.with_memory_space_constraint(array, pltpu.HBM) for array in arrays)

    sizes = (TILE,) * item_count
    starts = [j * TILE for j in range(item_count)]
    kept_shape = (visits * block_rows, rank), (visits * block_rows, user_rows)
    chunk, errors, used, *ready, users, rest, lists = call(
        functools.partial(first_kernel, item_count),
        "first_visit",
        (
            vmem((sizes[0], rank)),
            vmem(kept_shape[1]),
            vmem(kept_shape[0]),
            vmem((user_rows, rank), jnp.bfloat16),
            vmem((user_rows, rank), jnp.bfloat16),
            vmem((user_rows, rank)),
            vmem((block_rows - sizes[0], rank)),
            vmem(weights.shape, weights.dtype),
        ),
        [HBM] * 5,
        in_hbm(ids, counts, user_factors, item_factors, weights),
        flops=2 * unit * sizes[0],
        out_specs=(VMEM,) * 8,
        scratch_shapes=[
            pltpu.VMEM((sizes[0], rank), jnp.float32),
            pltpu.VMEM(weights.shape[1:], weights.dtype),
            pltpu.VMEM((TILE, user_rows), jnp.float32),
            pltpu.SMEM(ids.shape, jnp.int32),
            pltpu.SMEM(counts.shape, jnp.int32),
            pltpu.SemaphoreType.DMA((7,)),
        ],
    )
    kept = (errors, used)

    def dense_call(wanted, after):
        return call(
            functools.partial(dense_kernel, wanted, item_count),
            "dense_tiles",
            (jax.ShapeDtypeStruct((block_rows, user_rows), weights.dtype),) * len(wanted),
            [SMEM, SMEM] + [VMEM] * (1 + len(after)),
            (ids, counts, lists, *after),
            out_specs=(VMEM,) * len(wanted),
        )

    def visit_call(visit, j, dense, items, source, kept, after=(), joined=None, pieces=(TILE,)):
        more = 0 if joined is None else joined.shape[0]
        extra = (*after, *(() if joined is None else (joined,)))
        *rows, errors, used = call(
            functools.partial(
                visit_kernel, starts[j], source, visit * block_rows + starts[j], more, len(pieces)
            ),
            "visit_update",
            tuple(f32(more + piece, rank) for piece in pieces) + (f32(*kept_shape[1]), f32(*kept_shape[0])),
            [VMEM] * (6 + len(extra)),
            (*ready, dense, items, *kept, *extra),
            flops=2 * unit * TILE,
            out_specs=(VMEM,) * (2 + len(pieces)),
            input_output_aliases={4: len(pieces), 5: len(pieces) + 1},
        )
        return rows, (errors, used)

    chunks, returned = [chunk], []
    opening, dense = dense_call((0, 1), ())
    for j in range(1, item_count):
        (chunk,), kept = visit_call(0, j, opening, rest, starts[j] - sizes[0], kept)
        chunks.append(chunk)
    split = visits // 2 * block_rows
    left = None
    for visit in range(1, visits):
        if visit > 1:
            (dense,) = dense_call((visit,), kept)
        for j in range(item_count):
            after, joined, pieces = (), None, (TILE,)
            if visit == visits - 1:
                joined = left if j else None
                if j == 0 and item_count > 1 and FIRST_BACK:
                    pieces = (FIRST_BACK, TILE - FIRST_BACK)
                if j == item_count - 1:
                    total = call(
                        functools.partial(early_kernel, split),
                        "early_gradient",
                        f32(user_rows, rank),
                        [VMEM] * 2,
                        kept,
                        flops=unit * split,
                        out_specs=VMEM,
                    )
                    after = (total,)
            rows, kept = visit_call(
                visit, j, dense, shifted(chunks[j], "user", 1), 0, kept, after, joined, pieces
            )
            chunks[j] = left = rows[-1]
            if len(rows) > 1:
                returned.append(shifted(rows[0], "user", 1 - visits))
    returned.append(shifted(left, "user", 1 - visits))
    away = sections - 1
    total, *parts = call(
        functools.partial(gradient_kernel, split, sections),
        "user_gradient",
        (f32(user_rows, rank),) + (f32(user_rows // sections // PIECES, rank),) * (away * PIECES),
        [VMEM] * 3,
        (*kept, total),
        flops=unit * (visits * block_rows - split),
        out_specs=(VMEM,) * (1 + away * PIECES),
        input_output_aliases={2: 0},
    )

    received = [shifted(part, "isec", i // PIECES + 1) for i, part in enumerate(parts)]
    new_users = call(
        users_kernel,
        "new_users",
        f32(user_rows // sections, rank),
        [VMEM] * (2 + len(received)),
        (users, total, *received),
        limit=8 * MIB,
        out_specs=VMEM,
    )
    new_items = call(
        place_kernel,
        "place_items",
        f32(block_rows, rank),
        [VMEM] * len(returned),
        returned,
        limit=4 * MIB,
        out_specs=HBM,
        scratch_shapes=[pltpu.SemaphoreType.DMA((len(returned),))],
    )
    return new_users, new_items


def solution(mesh):
    return jax.shard_map(
        on_device,
        mesh=mesh,
        in_specs=(
            P("user", None),
            P(("user", "isec"), None),
            P("user", "isec", None, None, None, None),
            P("user", "isec", None, None),
            P("user", "isec", None),
        ),
        out_specs=(P(("user", "isec"), None), P(("user", "isec"), None)),
        check_vma=False,
    )
```

```python
import functools

import jax
import jax.numpy as jnp
from jax import lax
from jax.experimental import pallas as pl
from jax.experimental.pallas import tpu as pltpu
from jax.sharding import PartitionSpec as P

TILE = 128
SIZES = (64, 64, 64, 64)
GROUPS = ((0, 1, 2), (3,))
PIECES = 4
EARLY = 3

item_rate = 0.02
user_rate = 0.005
shrinkage = 0.1

MIB = 1 << 20
LIMIT = 16 * MIB
SMEM, HBM, VMEM = (pl.BlockSpec(memory_space=s) for s in (pltpu.SMEM, pltpu.HBM, pltpu.VMEM))


def shifted(block, axis, distance):
    count = lax.axis_size(axis)
    return lax.ppermute(block, axis, [((i - distance) % count, i) for i in range(count)])


def f32(*shape):
    return jax.ShapeDtypeStruct(shape, jnp.float32)


def halves(x):
    high = x.astype(jnp.bfloat16)
    return high, (x - high.astype(jnp.float32)).astype(jnp.bfloat16)


def dot(a, b, left, right):
    dims = (((left,), (right,)), ((), ()))
    return lax.dot_general(a, b, dims, preferred_element_type=jnp.float32)


def product(a, b, right):
    count = a[0].shape[0]
    both = dot(jnp.concatenate(a, axis=0), b[0], 1, right)
    return both[:count] + (both[count:] + dot(a[0], b[1], 1, right))


def errors_of(q, p, weights):
    return weights * (product(halves(q), p, 1) - 1.0)


def stepped(q, error, p):
    return q - item_rate * (product(halves(error), p, 0) + shrinkage * q)


def gradient(error, q):
    e, r = halves(error), halves(q)
    both = dot(jnp.concatenate(e, axis=0), jnp.concatenate([r[0], r[0]], axis=0), 0, 0)
    return both + dot(e[0], r[1], 0, 0)


def fill(dense, lists, ids, counts, visit, first, item_count):
    dense[...] = jnp.zeros_like(dense)
    rows = dense.shape[0]
    for n in range(lists.shape[0]):
        k = ids[visit, n]
        row = (k % item_count - first) * TILE

        @pl.when((n < counts[visit]) & (row >= 0) & (row < rows))
        def _():
            place = (
                pl.ds(pl.multiple_of(row, TILE), TILE),
                pl.ds(pl.multiple_of(k // item_count * TILE, TILE), TILE),
            )
            dense[place] = lists[n].astype(jnp.float32).T.astype(dense.dtype)


def first_kernel(item_count, ids, counts, users, items, weights, *refs):
    new_items, errors, used, high, low, p_rows, rest, lists, *refs = refs
    q_rows, first_lists, dense, own_ids, own_counts, arrived = refs
    pairs = [
        (ids, own_ids),
        (counts, own_counts),
        (weights.at[0], first_lists),
        (items.at[pl.ds(0, q_rows.shape[0])], q_rows),
        (users, p_rows),
        (weights, lists),
    ]
    pairs.append((items.at[pl.ds(q_rows.shape[0], rest.shape[0])], rest))
    copies = [pltpu.make_async_copy(*pair, arrived.at[i]) for i, pair in enumerate(pairs)]
    for copy in copies:
        copy.start()
    for copy in copies[:3]:
        copy.wait()
    fill(dense, first_lists, own_ids, own_counts, 0, 0, item_count)
    copies[3].wait()
    q = q_rows[...]
    copies[4].wait()
    p = halves(p_rows[...])
    high[...], low[...] = p
    e = errors_of(q, p, dense[pl.ds(0, q.shape[0]), :])
    new_items[...] = stepped(q, e, p)
    errors[pl.ds(0, q.shape[0]), :] = e
    used[pl.ds(0, q.shape[0]), :] = q
    for copy in copies[5:]:
        copy.wait()


def dense_kernel(wanted, item_count, ids, counts, weights, *refs):
    for visit, target in zip(wanted, refs[-len(wanted) :], strict=True):
        fill(target, weights.at[visit], ids, counts, visit, 0, item_count)


def visit_kernel(first, count, source, kept, joined, high, low, dense, items, *refs):
    new_items, errors, used = refs[-3:]
    start = 0
    for chunk in refs[len(refs) - 3 - joined : -3]:
        new_items[pl.ds(start, chunk.shape[0]), :] = chunk[...]
        start += chunk.shape[0]
    q, p = items[pl.ds(source, count), :], (high[...], low[...])
    e = errors_of(q, p, dense[pl.ds(first, count), :].astype(jnp.float32))
    new_items[pl.ds(start, count), :] = stepped(q, e, p)
    rows = pl.ds(kept, count)
    errors[rows, :] = e
    used[rows, :] = q


def early_kernel(split, errors, used, total):
    total[...] = gradient(errors[:split, :], used[:split, :])


def gradient_kernel(split, shares, errors, used, total, new_total, *parts):
    new_total[...] = total[...] + gradient(errors[split:, :], used[split:, :])
    share = total.shape[0] // shares
    for i, part in enumerate(parts):
        away, piece = i // PIECES + 1, i % PIECES
        size = part.shape[0]
        start = lax.rem(lax.axis_index("isec") + away, shares) * share + piece * size
        part[...] = new_total[pl.ds(pl.multiple_of(start, size), size), :]


def users_kernel(users, total, *refs):
    *received, new_users = refs
    share = new_users.shape[0]
    size = share // PIECES
    for piece in range(PIECES):
        start = lax.axis_index("isec") * share + piece * size
        rows = pl.ds(pl.multiple_of(start, size), size)
        summed = total[rows, :]
        for term in received[piece::PIECES]:
            summed = summed + term[...]
        p = users[rows, :]
        new_users[pl.ds(piece * size, size), :] = p - user_rate * (summed + shrinkage * p)


def place_kernel(*refs):
    *chunks, whole, moved = refs
    start, stores = 0, []
    for i, chunk in enumerate(chunks):
        target = whole.at[pl.ds(start, chunk.shape[0])]
        stores.append(pltpu.make_async_copy(chunk, target, moved.at[i]))
        start += chunk.shape[0]
    for store in stores:
        store.start()
    for store in stores:
        store.wait()


def call(kernel, name, out_shape, in_specs, args, flops=0, limit=LIMIT, **more):
    cost = pl.CostEstimate(flops=flops, bytes_accessed=MIB, transcendentals=0)
    return pl.pallas_call(
        kernel,
        name=name,
        out_shape=out_shape,
        in_specs=in_specs,
        cost_estimate=cost,
        compiler_params=pltpu.CompilerParams(vmem_limit_bytes=limit),
        **more,
    )(*args)


def on_device(user_factors, item_factors, confidence, tile_ids, tile_counts):
    visits = confidence.shape[2]
    user_rows, rank = user_factors.shape
    block_rows = item_factors.shape[0]
    item_count = block_rows // TILE
    sections = lax.axis_size("isec")
    weights, ids, counts = confidence[0, 0], tile_ids[0, 0], tile_counts[0, 0]
    unit = 2 * 3 * user_rows * rank

    def vmem(shape, dtype=jnp.float32):
        return pltpu.VMEM(shape, dtype)

    def in_hbm(*arrays):
        return tuple(pltpu.with_memory_space_constraint(array, pltpu.HBM) for array in arrays)

    sizes = SIZES if sum(SIZES) == block_rows else (TILE,) * item_count
    starts = [sum(sizes[:i]) for i in range(len(sizes))]
    kept_shape = (visits * block_rows, rank), (visits * block_rows, user_rows)
    chunk, errors, used, *ready, users, rest, lists = call(
        functools.partial(first_kernel, item_count),
        "first_visit",
        (
            vmem((sizes[0], rank)),
            vmem(kept_shape[1]),
            vmem(kept_shape[0]),
            vmem((user_rows, rank), jnp.bfloat16),
            vmem((user_rows, rank), jnp.bfloat16),
            vmem((user_rows, rank)),
            vmem((block_rows - sizes[0], rank)),
            vmem(weights.shape, weights.dtype),
        ),
        [HBM] * 5,
        in_hbm(ids, counts, user_factors, item_factors, weights),
        flops=2 * unit * sizes[0],
        out_specs=(VMEM,) * 8,
        scratch_shapes=[
            pltpu.VMEM((sizes[0], rank), jnp.float32),
            pltpu.VMEM(weights.shape[1:], weights.dtype),
            pltpu.VMEM((TILE, user_rows), jnp.float32),
            pltpu.SMEM(ids.shape, jnp.int32),
            pltpu.SMEM(counts.shape, jnp.int32),
            pltpu.SemaphoreType.DMA((7,)),
        ],
    )
    kept = (errors, used)

    def dense_call(wanted, after):
        return call(
            functools.partial(dense_kernel, wanted, item_count),
            "dense_tiles",
            (jax.ShapeDtypeStruct((block_rows, user_rows), weights.dtype),) * len(wanted),
            [SMEM, SMEM] + [VMEM] * (1 + len(after)),
            (ids, counts, lists, *after),
            out_specs=(VMEM,) * len(wanted),
        )

    def visit_call(visit, c, dense, items, source, kept, after=(), joined=()):
        start, size = starts[c], sizes[c]
        return call(
            functools.partial(visit_kernel, start, size, source, visit * block_rows + start, len(joined)),
            "visit_update",
            (
                f32(size + sum(chunk.shape[0] for chunk in joined), rank),
                f32(*kept_shape[1]),
                f32(*kept_shape[0]),
            ),
            [VMEM] * (6 + len(after) + len(joined)),
            (*ready, dense, items, *kept, *after, *joined),
            flops=2 * unit * size,
            out_specs=(VMEM,) * 3,
            input_output_aliases={4: 1, 5: 2},
        )

    groups = GROUPS if len(sizes) == GROUPS[-1][-1] + 1 else [(c,) for c in range(len(sizes))]
    chunks, returned = [chunk], []
    opening, dense = dense_call((0, 1), ())
    for c in range(1, len(sizes)):
        chunk, *kept = visit_call(0, c, opening, rest, starts[c] - sizes[0], kept)
        chunks.append(chunk)
    split = visits // 2 * block_rows
    for visit in range(1, visits):
        if visit > 1:
            (dense,) = dense_call((visit,), kept)
        for c in range(len(sizes)):
            last = visit == visits - 1
            after = ()
            if last and c == min(EARLY, len(sizes) - 1):
                total = call(
                    functools.partial(early_kernel, split),
                    "early_gradient",
                    f32(user_rows, rank),
                    [VMEM] * 2,
                    kept,
                    flops=unit * split,
                    out_specs=VMEM,
                )
                after = (total,)
            group = next(group for group in groups if c in group)
            joined = [chunks[i] for i in group[:-1]] if last and c == group[-1] else ()
            chunks[c], *kept = visit_call(
                visit, c, dense, shifted(chunks[c], "user", 1), 0, kept, after, joined
            )
            if last and c == group[-1]:
                returned.append(shifted(chunks[c], "user", 1 - visits))
    away = sections - 1
    total, *parts = call(
        functools.partial(gradient_kernel, split, sections),
        "user_gradient",
        (f32(user_rows, rank),) + (f32(user_rows // sections // PIECES, rank),) * (away * PIECES),
        [VMEM] * 3,
        (*kept, total),
        flops=unit * (visits * block_rows - split),
        out_specs=(VMEM,) * (1 + away * PIECES),
        input_output_aliases={2: 0},
    )

    received = [shifted(part, "isec", i // PIECES + 1) for i, part in enumerate(parts)]
    new_users = call(
        users_kernel,
        "new_users",
        f32(user_rows // sections, rank),
        [VMEM] * (2 + len(received)),
        (users, total, *received),
        limit=8 * MIB,
        out_specs=VMEM,
    )
    new_items = call(
        place_kernel,
        "place_items",
        f32(block_rows, rank),
        [VMEM] * len(returned),
        returned,
        limit=4 * MIB,
        out_specs=HBM,
        scratch_shapes=[pltpu.SemaphoreType.DMA((len(returned),))],
    )
    return new_users, new_items


def solution(mesh):
    return jax.shard_map(
        on_device,
        mesh=mesh,
        in_specs=(
            P("user", None),
            P(("user", "isec"), None),
            P("user", "isec", None, None, None, None),
            P("user", "isec", None, None),
            P("user", "isec", None),
        ),
        out_specs=(P(("user", "isec"), None), P(("user", "isec"), None)),
        check_vma=False,
    )
```

```python
import functools

import jax
import jax.numpy as jnp
from jax import lax
from jax.experimental import pallas as pl
from jax.experimental.pallas import tpu as pltpu
from jax.sharding import PartitionSpec as P

TILE = 128
SIZES = (64, 64, 64, 64)
GROUPS = ((0, 1, 2), (3,))
PIECES = 4
EARLY = 1

item_rate = 0.02
user_rate = 0.005
shrinkage = 0.1

MIB = 1 << 20
LIMIT = 16 * MIB
SMEM, HBM, VMEM = (pl.BlockSpec(memory_space=s) for s in (pltpu.SMEM, pltpu.HBM, pltpu.VMEM))


def shifted(block, axis, distance):
    count = lax.axis_size(axis)
    return lax.ppermute(block, axis, [((i - distance) % count, i) for i in range(count)])


def f32(*shape):
    return jax.ShapeDtypeStruct(shape, jnp.float32)


def halves(x):
    high = x.astype(jnp.bfloat16)
    return high, (x - high.astype(jnp.float32)).astype(jnp.bfloat16)


def dot(a, b, left, right):
    dims = (((left,), (right,)), ((), ()))
    return lax.dot_general(a, b, dims, preferred_element_type=jnp.float32)


def product(a, b, right):
    count = a[0].shape[0]
    both = dot(jnp.concatenate(a, axis=0), b[0], 1, right)
    return both[:count] + (both[count:] + dot(a[0], b[1], 1, right))


def errors_of(q, p, weights):
    return weights * (product(halves(q), p, 1) - 1.0)


def stepped(q, error, p):
    return q - item_rate * (product(halves(error), p, 0) + shrinkage * q)


def gradient(error, q):
    e, r = halves(error), halves(q)
    both = dot(jnp.concatenate(e, axis=0), jnp.concatenate([r[0], r[0]], axis=0), 0, 0)
    return both + dot(e[0], r[1], 0, 0)


def fill(dense, lists, ids, counts, visit, first, item_count):
    dense[...] = jnp.zeros_like(dense)
    rows = dense.shape[0]
    for n in range(lists.shape[0]):
        k = ids[visit, n]
        row = (k % item_count - first) * TILE

        @pl.when((n < counts[visit]) & (row >= 0) & (row < rows))
        def _():
            place = (
                pl.ds(pl.multiple_of(row, TILE), TILE),
                pl.ds(pl.multiple_of(k // item_count * TILE, TILE), TILE),
            )
            dense[place] = lists[n].T.astype(dense.dtype)


def first_kernel(item_count, ids, counts, users, items, weights, *refs):
    new_items, errors, used, high, low, p_rows, rest, lists, *refs = refs
    q_rows, first_lists, dense, own_ids, own_counts, arrived = refs
    pairs = [
        (ids, own_ids),
        (counts, own_counts),
        (weights.at[0], first_lists),
        (items.at[pl.ds(0, q_rows.shape[0])], q_rows),
        (users, p_rows),
        (weights, lists),
    ]
    pairs.append((items.at[pl.ds(q_rows.shape[0], rest.shape[0])], rest))
    copies = [pltpu.make_async_copy(*pair, arrived.at[i]) for i, pair in enumerate(pairs)]
    for copy in copies:
        copy.start()
    for copy in copies[:3]:
        copy.wait()
    fill(dense, first_lists, own_ids, own_counts, 0, 0, item_count)
    copies[3].wait()
    q = q_rows[...]
    copies[4].wait()
    p = halves(p_rows[...])
    high[...], low[...] = p
    e = errors_of(q, p, dense[pl.ds(0, q.shape[0]), :])
    new_items[...] = stepped(q, e, p)
    errors[pl.ds(0, q.shape[0]), :] = e
    used[pl.ds(0, q.shape[0]), :] = q
    for copy in copies[5:]:
        copy.wait()


def dense_kernel(wanted, item_count, ids, counts, weights, *refs):
    for (visit, tile), target in zip(wanted, refs[-len(wanted) :], strict=True):
        fill(target, weights.at[visit], ids, counts, visit, tile, item_count)


def visit_kernel(first, count, source, kept, joined, high, low, dense, items, *refs):
    new_items, errors, used = refs[-3:]
    start = 0
    for chunk in refs[len(refs) - 3 - joined : -3]:
        new_items[pl.ds(start, chunk.shape[0]), :] = chunk[...]
        start += chunk.shape[0]
    q, p = items[pl.ds(source, count), :], (high[...], low[...])
    e = errors_of(q, p, dense[pl.ds(first, count), :].astype(jnp.float32))
    new_items[pl.ds(start, count), :] = stepped(q, e, p)
    rows = pl.ds(kept, count)
    errors[rows, :] = e
    used[rows, :] = q


def early_kernel(split, errors, used, total):
    total[...] = gradient(errors[:split, :], used[:split, :])


def gradient_kernel(split, shares, errors, used, total, new_total, *parts):
    new_total[...] = total[...] + gradient(errors[split:, :], used[split:, :])
    share = total.shape[0] // shares
    for i, part in enumerate(parts):
        away, piece = i // PIECES + 1, i % PIECES
        size = part.shape[0]
        start = lax.rem(lax.axis_index("isec") + away, shares) * share + piece * size
        part[...] = new_total[pl.ds(pl.multiple_of(start, size), size), :]


def users_kernel(users, total, *refs):
    *received, new_users = refs
    share = new_users.shape[0]
    size = share // PIECES
    for piece in range(PIECES):
        start = lax.axis_index("isec") * share + piece * size
        rows = pl.ds(pl.multiple_of(start, size), size)
        summed = total[rows, :]
        for term in received[piece::PIECES]:
            summed = summed + term[...]
        p = users[rows, :]
        new_users[pl.ds(piece * size, size), :] = p - user_rate * (summed + shrinkage * p)


def place_kernel(*refs):
    *chunks, whole, moved = refs
    start, stores = 0, []
    for i, chunk in enumerate(chunks):
        target = whole.at[pl.ds(start, chunk.shape[0])]
        stores.append(pltpu.make_async_copy(chunk, target, moved.at[i]))
        start += chunk.shape[0]
    for store in stores:
        store.start()
    for store in stores:
        store.wait()


def call(kernel, name, out_shape, in_specs, args, flops=0, limit=LIMIT, **more):
    cost = pl.CostEstimate(flops=flops, bytes_accessed=MIB, transcendentals=0)
    return pl.pallas_call(
        kernel,
        name=name,
        out_shape=out_shape,
        in_specs=in_specs,
        cost_estimate=cost,
        compiler_params=pltpu.CompilerParams(vmem_limit_bytes=limit),
        **more,
    )(*args)


def on_device(user_factors, item_factors, confidence, tile_ids, tile_counts):
    visits = confidence.shape[2]
    user_rows, rank = user_factors.shape
    block_rows = item_factors.shape[0]
    item_count = block_rows // TILE
    sections = lax.axis_size("isec")
    weights, ids, counts = confidence[0, 0], tile_ids[0, 0], tile_counts[0, 0]
    unit = 2 * 3 * user_rows * rank

    def vmem(shape, dtype=jnp.float32):
        return pltpu.VMEM(shape, dtype)

    def in_hbm(*arrays):
        return tuple(pltpu.with_memory_space_constraint(array, pltpu.HBM) for array in arrays)

    sizes = SIZES if sum(SIZES) == block_rows else (TILE,) * item_count
    starts = [sum(sizes[:i]) for i in range(len(sizes))]
    kept_shape = (visits * block_rows, rank), (visits * block_rows, user_rows)
    chunk, errors, used, *ready, users, rest, lists = call(
        functools.partial(first_kernel, item_count),
        "first_visit",
        (
            vmem((sizes[0], rank)),
            vmem(kept_shape[1]),
            vmem(kept_shape[0]),
            vmem((user_rows, rank), jnp.bfloat16),
            vmem((user_rows, rank), jnp.bfloat16),
            vmem((user_rows, rank)),
            vmem((block_rows - sizes[0], rank)),
            vmem(weights.shape, weights.dtype),
        ),
        [HBM] * 5,
        in_hbm(ids, counts, user_factors, item_factors, weights),
        flops=2 * unit * sizes[0],
        out_specs=(VMEM,) * 8,
        scratch_shapes=[
            pltpu.VMEM((sizes[0], rank), jnp.float32),
            pltpu.VMEM(weights.shape[1:], weights.dtype),
            pltpu.VMEM((TILE, user_rows), jnp.float32),
            pltpu.SMEM(ids.shape, jnp.int32),
            pltpu.SMEM(counts.shape, jnp.int32),
            pltpu.SemaphoreType.DMA((7,)),
        ],
    )
    kept = (errors, used)

    def dense_call(wanted, after):
        return call(
            functools.partial(dense_kernel, wanted, item_count),
            "dense_tiles",
            (jax.ShapeDtypeStruct((TILE, user_rows), weights.dtype),) * len(wanted),
            [SMEM, SMEM] + [VMEM] * (1 + len(after)),
            (ids, counts, lists, *after),
            out_specs=(VMEM,) * len(wanted),
        )

    def visit_call(visit, c, dense, items, source, kept, after=(), joined=()):
        start, size = starts[c], sizes[c]
        return call(
            functools.partial(visit_kernel, start % TILE, size, source, visit * block_rows + start, len(joined)),
            "visit_update",
            (
                f32(size + sum(chunk.shape[0] for chunk in joined), rank),
                f32(*kept_shape[1]),
                f32(*kept_shape[0]),
            ),
            [VMEM] * (6 + len(after) + len(joined)),
            (*ready, dense, items, *kept, *after, *joined),
            flops=2 * unit * size,
            out_specs=(VMEM,) * 3,
            input_output_aliases={4: 1, 5: 2},
        )

    groups = GROUPS if len(sizes) == GROUPS[-1][-1] + 1 else [(c,) for c in range(len(sizes))]
    chunks, returned = [chunk], []
    wanted = [(0, j) for j in range(item_count)] + [(1, 0)]
    dense = dict(zip(wanted, dense_call(wanted, ()), strict=True))
    for c in range(1, len(sizes)):
        chunk, *kept = visit_call(0, c, dense[0, starts[c] // TILE], rest, starts[c] - sizes[0], kept)
        chunks.append(chunk)
    split = visits // 2 * block_rows
    for visit in range(1, visits):
        for c in range(len(sizes)):
            tile = (visit, starts[c] // TILE)
            if tile not in dense:
                (dense[tile],) = dense_call([tile], kept)
            last = visit == visits - 1
            after = ()
            if last and c == min(EARLY, len(sizes) - 1):
                total = call(
                    functools.partial(early_kernel, split),
                    "early_gradient",
                    f32(user_rows, rank),
                    [VMEM] * 2,
                    kept,
                    flops=unit * split,
                    out_specs=VMEM,
                )
                after = (total,)
            group = next(group for group in groups if c in group)
            joined = [chunks[i] for i in group[:-1]] if last and c == group[-1] else ()
            chunks[c], *kept = visit_call(
                visit, c, dense[tile], shifted(chunks[c], "user", 1), 0, kept, after, joined
            )
            if last and c == group[-1]:
                returned.append(shifted(chunks[c], "user", 1 - visits))
    away = sections - 1
    total, *parts = call(
        functools.partial(gradient_kernel, split, sections),
        "user_gradient",
        (f32(user_rows, rank),) + (f32(user_rows // sections // PIECES, rank),) * (away * PIECES),
        [VMEM] * 3,
        (*kept, total),
        flops=unit * (visits * block_rows - split),
        out_specs=(VMEM,) * (1 + away * PIECES),
        input_output_aliases={2: 0},
    )

    received = [shifted(part, "isec", i // PIECES + 1) for i, part in enumerate(parts)]
    new_users = call(
        users_kernel,
        "new_users",
        f32(user_rows // sections, rank),
        [VMEM] * (2 + len(received)),
        (users, total, *received),
        limit=8 * MIB,
        out_specs=VMEM,
    )
    new_items = call(
        place_kernel,
        "place_items",
        f32(block_rows, rank),
        [VMEM] * len(returned),
        returned,
        limit=4 * MIB,
        out_specs=HBM,
        scratch_shapes=[pltpu.SemaphoreType.DMA((len(returned),))],
    )
    return new_users, new_items


def solution(mesh):
    return jax.shard_map(
        on_device,
        mesh=mesh,
        in_specs=(
            P("user", None),
            P(("user", "isec"), None),
            P("user", "isec", None, None, None, None),
            P("user", "isec", None, None),
            P("user", "isec", None),
        ),
        out_specs=(P(("user", "isec"), None), P(("user", "isec"), None)),
        check_vma=False,
    )
```

```python
import functools

import jax
import jax.numpy as jnp
from jax import lax
from jax.experimental import pallas as pl
from jax.experimental.pallas import tpu as pltpu
from jax.sharding import PartitionSpec as P

TILE = 128
ROWS = TILE // 2
PIECES = 4
EARLY = 1

item_rate = 0.02
user_rate = 0.005
shrinkage = 0.1

MIB = 1 << 20
LIMIT = 16 * MIB
SMEM, HBM, VMEM = (pl.BlockSpec(memory_space=s) for s in (pltpu.SMEM, pltpu.HBM, pltpu.VMEM))


def shifted(block, axis, distance):
    count = lax.axis_size(axis)
    return lax.ppermute(block, axis, [((i - distance) % count, i) for i in range(count)])


def f32(*shape):
    return jax.ShapeDtypeStruct(shape, jnp.float32)


def halves(x):
    high = x.astype(jnp.bfloat16)
    return high, (x - high.astype(jnp.float32)).astype(jnp.bfloat16)


def dot(a, b, left, right):
    dims = (((left,), (right,)), ((), ()))
    return lax.dot_general(a, b, dims, preferred_element_type=jnp.float32)


def product(a, b, right):
    count = a[0].shape[0]
    both = dot(jnp.concatenate(a, axis=0), b[0], 1, right)
    return both[:count] + (both[count:] + dot(a[0], b[1], 1, right))


def errors_of(q, p, weights):
    return weights * (product(halves(q), p, 1) - 1.0)


def stepped(q, error, p):
    return q - item_rate * (product(halves(error), p, 0) + shrinkage * q)


def gradient(error, q):
    e, r = halves(error), halves(q)
    both = dot(jnp.concatenate(e, axis=0), jnp.concatenate([r[0], r[0]], axis=0), 0, 0)
    return both + dot(e[0], r[1], 0, 0)


def fill(dense, lists, ids, counts, visit, first, item_count):
    dense[...] = jnp.zeros_like(dense)
    rows = dense.shape[0]
    for n in range(lists.shape[0]):
        k = ids[visit, n]
        row = (k % item_count - first) * TILE

        @pl.when((n < counts[visit]) & (row >= 0) & (row < rows))
        def _():
            place = (
                pl.ds(pl.multiple_of(row, TILE), TILE),
                pl.ds(pl.multiple_of(k // item_count * TILE, TILE), TILE),
            )
            dense[place] = lists[n].T.astype(dense.dtype)


def first_kernel(item_count, ids, counts, users, items, weights, *refs):
    new_items, errors, used, high, low, p_rows, rest, lists, *refs = refs
    q_rows, first_lists, dense, own_ids, own_counts, arrived = refs
    pairs = [
        (ids, own_ids),
        (counts, own_counts),
        (weights.at[0], first_lists),
        (items.at[pl.ds(0, q_rows.shape[0])], q_rows),
        (users, p_rows),
        (weights, lists),
    ]
    pairs.append((items.at[pl.ds(q_rows.shape[0], rest.shape[0])], rest))
    copies = [pltpu.make_async_copy(*pair, arrived.at[i]) for i, pair in enumerate(pairs)]
    for copy in copies:
        copy.start()
    for copy in copies[:3]:
        copy.wait()
    fill(dense, first_lists, own_ids, own_counts, 0, 0, item_count)
    copies[3].wait()
    q = q_rows[...]
    copies[4].wait()
    p = halves(p_rows[...])
    high[...], low[...] = p
    e = errors_of(q, p, dense[pl.ds(0, q.shape[0]), :])
    new_items[...] = stepped(q, e, p)
    errors[pl.ds(0, q.shape[0]), :] = e
    used[pl.ds(0, q.shape[0]), :] = q
    for copy in copies[5:]:
        copy.wait()


def dense_kernel(wanted, item_count, ids, counts, weights, *refs):
    for (visit, tile), target in zip(wanted, refs[-len(wanted) :], strict=True):
        fill(target, weights.at[visit], ids, counts, visit, tile, item_count)


def visit_kernel(first, count, source, kept, joined, high, low, dense, items, *refs):
    new_items, errors, used = refs[-3:]
    start = 0
    for chunk in refs[len(refs) - 3 - joined : -3]:
        new_items[pl.ds(start, chunk.shape[0]), :] = chunk[...]
        start += chunk.shape[0]
    q, p = items[pl.ds(source, count), :], (high[...], low[...])
    e = errors_of(q, p, dense[pl.ds(first, count), :].astype(jnp.float32))
    new_items[pl.ds(start, count), :] = stepped(q, e, p)
    rows = pl.ds(kept, count)
    errors[rows, :] = e
    used[rows, :] = q


def early_kernel(split, errors, used, total):
    total[...] = gradient(errors[:split, :], used[:split, :])


def gradient_kernel(split, shares, errors, used, total, new_total, *parts):
    new_total[...] = total[...] + gradient(errors[split:, :], used[split:, :])
    share = total.shape[0] // shares
    for i, part in enumerate(parts):
        away, piece = i // PIECES + 1, i % PIECES
        size = part.shape[0]
        start = lax.rem(lax.axis_index("isec") + away, shares) * share + piece * size
        part[...] = new_total[pl.ds(pl.multiple_of(start, size), size), :]


def users_kernel(users, total, *refs):
    *received, new_users = refs
    share = new_users.shape[0]
    size = share // PIECES
    for piece in range(PIECES):
        start = lax.axis_index("isec") * share + piece * size
        rows = pl.ds(pl.multiple_of(start, size), size)
        summed = total[rows, :]
        for term in received[piece::PIECES]:
            summed = summed + term[...]
        p = users[rows, :]
        new_users[pl.ds(piece * size, size), :] = p - user_rate * (summed + shrinkage * p)


def place_kernel(*refs):
    *chunks, whole, moved = refs
    start, stores = 0, []
    for i, chunk in enumerate(chunks):
        target = whole.at[pl.ds(start, chunk.shape[0])]
        stores.append(pltpu.make_async_copy(chunk, target, moved.at[i]))
        start += chunk.shape[0]
    for store in stores:
        store.start()
    for store in stores:
        store.wait()


def call(kernel, name, out_shape, in_specs, args, flops=0, limit=LIMIT, **more):
    cost = pl.CostEstimate(flops=flops, bytes_accessed=MIB, transcendentals=0)
    return pl.pallas_call(
        kernel,
        name=name,
        out_shape=out_shape,
        in_specs=in_specs,
        cost_estimate=cost,
        compiler_params=pltpu.CompilerParams(vmem_limit_bytes=limit),
        **more,
    )(*args)


def on_device(user_factors, item_factors, confidence, tile_ids, tile_counts):
    visits = confidence.shape[2]
    user_rows, rank = user_factors.shape
    block_rows = item_factors.shape[0]
    item_count = block_rows // TILE
    sections = lax.axis_size("isec")
    weights, ids, counts = confidence[0, 0], tile_ids[0, 0], tile_counts[0, 0]
    unit = 2 * 3 * user_rows * rank

    def vmem(shape, dtype=jnp.float32):
        return pltpu.VMEM(shape, dtype)

    def in_hbm(*arrays):
        return tuple(pltpu.with_memory_space_constraint(array, pltpu.HBM) for array in arrays)

    sizes = (ROWS,) * (block_rows // ROWS)
    starts = [sum(sizes[:i]) for i in range(len(sizes))]
    kept_shape = (visits * block_rows, rank), (visits * block_rows, user_rows)
    chunk, errors, used, *ready, users, rest, lists = call(
        functools.partial(first_kernel, item_count),
        "first_visit",
        (
            vmem((sizes[0], rank)),
            vmem(kept_shape[1]),
            vmem(kept_shape[0]),
            vmem((user_rows, rank), jnp.bfloat16),
            vmem((user_rows, rank), jnp.bfloat16),
            vmem((user_rows, rank)),
            vmem((block_rows - sizes[0], rank)),
            vmem(weights.shape, weights.dtype),
        ),
        [HBM] * 5,
        in_hbm(ids, counts, user_factors, item_factors, weights),
        flops=2 * unit * sizes[0],
        out_specs=(VMEM,) * 8,
        scratch_shapes=[
            pltpu.VMEM((sizes[0], rank), jnp.float32),
            pltpu.VMEM(weights.shape[1:], weights.dtype),
            pltpu.VMEM((TILE, user_rows), jnp.float32),
            pltpu.SMEM(ids.shape, jnp.int32),
            pltpu.SMEM(counts.shape, jnp.int32),
            pltpu.SemaphoreType.DMA((7,)),
        ],
    )
    kept = (errors, used)

    def dense_call(wanted, after):
        return call(
            functools.partial(dense_kernel, wanted, item_count),
            "dense_tiles",
            (jax.ShapeDtypeStruct((TILE, user_rows), weights.dtype),) * len(wanted),
            [SMEM, SMEM] + [VMEM] * (1 + len(after)),
            (ids, counts, lists, *after),
            out_specs=(VMEM,) * len(wanted),
        )

    def visit_call(visit, c, dense, items, source, kept, after=(), joined=()):
        start, size = starts[c], sizes[c]
        return call(
            functools.partial(visit_kernel, start % TILE, size, source, visit * block_rows + start, len(joined)),
            "visit_update",
            (
                f32(size + sum(chunk.shape[0] for chunk in joined), rank),
                f32(*kept_shape[1]),
                f32(*kept_shape[0]),
            ),
            [VMEM] * (6 + len(after) + len(joined)),
            (*ready, dense, items, *kept, *after, *joined),
            flops=2 * unit * size,
            out_specs=(VMEM,) * 3,
            input_output_aliases={4: 1, 5: 2},
        )

    groups = (tuple(range(len(sizes) - 1)), (len(sizes) - 1,))
    chunks, returned = [chunk], []
    wanted = [(0, j) for j in range(item_count)] + [(1, 0)]
    dense = dict(zip(wanted, dense_call(wanted, ()), strict=True))
    for c in range(1, len(sizes)):
        chunk, *kept = visit_call(0, c, dense[0, starts[c] // TILE], rest, starts[c] - sizes[0], kept)
        chunks.append(chunk)
    split = visits // 2 * block_rows
    for visit in range(1, visits):
        for c in range(len(sizes)):
            tile = (visit, starts[c] // TILE)
            if tile not in dense:
                (dense[tile],) = dense_call([tile], kept)
            last = visit == visits - 1
            after = ()
            if last and c == min(EARLY, len(sizes) - 1):
                total = call(
                    functools.partial(early_kernel, split),
                    "early_gradient",
                    f32(user_rows, rank),
                    [VMEM] * 2,
                    kept,
                    flops=unit * split,
                    out_specs=VMEM,
                )
                after = (total,)
            group = next(group for group in groups if c in group)
            joined = [chunks[i] for i in group[:-1]] if last and c == group[-1] else ()
            chunks[c], *kept = visit_call(
                visit, c, dense[tile], shifted(chunks[c], "user", 1), 0, kept, after, joined
            )
            if last and c == group[-1]:
                returned.append(shifted(chunks[c], "user", 1 - visits))
    away = sections - 1
    total, *parts = call(
        functools.partial(gradient_kernel, split, sections),
        "user_gradient",
        (f32(user_rows, rank),) + (f32(user_rows // sections // PIECES, rank),) * (away * PIECES),
        [VMEM] * 3,
        (*kept, total),
        flops=unit * (visits * block_rows - split),
        out_specs=(VMEM,) * (1 + away * PIECES),
        input_output_aliases={2: 0},
    )

    received = [shifted(part, "isec", i // PIECES + 1) for i, part in enumerate(parts)]
    new_users = call(
        users_kernel,
        "new_users",
        f32(user_rows // sections, rank),
        [VMEM] * (2 + len(received)),
        (users, total, *received),
        limit=8 * MIB,
        out_specs=VMEM,
    )
    new_items = call(
        place_kernel,
        "place_items",
        f32(block_rows, rank),
        [VMEM] * len(returned),
        returned,
        limit=4 * MIB,
        out_specs=HBM,
        scratch_shapes=[pltpu.SemaphoreType.DMA((len(returned),))],
    )
    return new_users, new_items


def solution(mesh):
    return jax.shard_map(
        on_device,
        mesh=mesh,
        in_specs=(
            P("user", None),
            P(("user", "isec"), None),
            P("user", "isec", None, None, None, None),
            P("user", "isec", None, None),
            P("user", "isec", None),
        ),
        out_specs=(P(("user", "isec"), None), P(("user", "isec"), None)),
        check_vma=False,
    )
```

```python
import functools

import jax
import jax.numpy as jnp
from jax import lax
from jax.experimental import pallas as pl
from jax.experimental.pallas import tpu as pltpu
from jax.sharding import PartitionSpec as P

TILE = 128
ROWS = TILE // 2
PIECES = 2
EARLY = 1

item_rate = 0.02
user_rate = 0.005
shrinkage = 0.1

MIB = 1 << 20
LIMIT = 16 * MIB
SMEM, HBM, VMEM = (pl.BlockSpec(memory_space=s) for s in (pltpu.SMEM, pltpu.HBM, pltpu.VMEM))


def shifted(block, axis, distance):
    count = lax.axis_size(axis)
    return lax.ppermute(block, axis, [((i - distance) % count, i) for i in range(count)])


def f32(*shape):
    return jax.ShapeDtypeStruct(shape, jnp.float32)


def halves(x):
    high = x.astype(jnp.bfloat16)
    return high, (x - high.astype(jnp.float32)).astype(jnp.bfloat16)


def dot(a, b, left, right):
    dims = (((left,), (right,)), ((), ()))
    return lax.dot_general(a, b, dims, preferred_element_type=jnp.float32)


def product(a, b, right):
    count = a[0].shape[0]
    both = dot(jnp.concatenate(a, axis=0), b[0], 1, right)
    return both[:count] + (both[count:] + dot(a[0], b[1], 1, right))


def errors_of(q, p, weights):
    return weights * (product(halves(q), p, 1) - 1.0)


def stepped(q, error, p):
    return q - item_rate * (product(halves(error), p, 0) + shrinkage * q)


def gradient(error, q):
    e, r = halves(error), halves(q)
    both = dot(jnp.concatenate(e, axis=0), jnp.concatenate([r[0], r[0]], axis=0), 0, 0)
    return both + dot(e[0], r[1], 0, 0)


def fill(dense, lists, ids, counts, visit, first, item_count):
    dense[...] = jnp.zeros_like(dense)
    rows = dense.shape[0]
    for n in range(lists.shape[0]):
        k = ids[visit, n]
        row = (k % item_count - first) * TILE

        @pl.when((n < counts[visit]) & (row >= 0) & (row < rows))
        def _():
            place = (
                pl.ds(pl.multiple_of(row, TILE), TILE),
                pl.ds(pl.multiple_of(k // item_count * TILE, TILE), TILE),
            )
            dense[place] = lists[n].T.astype(dense.dtype)


def first_kernel(item_count, ids, counts, users, items, weights, *refs):
    new_items, errors, used, high, low, p_rows, rest, lists, *refs = refs
    q_rows, first_lists, dense, own_ids, own_counts, arrived = refs
    pairs = [
        (ids, own_ids),
        (counts, own_counts),
        (weights.at[0], first_lists),
        (items.at[pl.ds(0, q_rows.shape[0])], q_rows),
        (users, p_rows),
        (weights, lists),
    ]
    pairs.append((items.at[pl.ds(q_rows.shape[0], rest.shape[0])], rest))
    copies = [pltpu.make_async_copy(*pair, arrived.at[i]) for i, pair in enumerate(pairs)]
    for copy in copies:
        copy.start()
    for copy in copies[:3]:
        copy.wait()
    fill(dense, first_lists, own_ids, own_counts, 0, 0, item_count)
    copies[3].wait()
    q = q_rows[...]
    copies[4].wait()
    p = halves(p_rows[...])
    high[...], low[...] = p
    e = errors_of(q, p, dense[pl.ds(0, q.shape[0]), :])
    new_items[...] = stepped(q, e, p)
    errors[pl.ds(0, q.shape[0]), :] = e
    used[pl.ds(0, q.shape[0]), :] = q
    for copy in copies[5:]:
        copy.wait()


def dense_kernel(wanted, item_count, ids, counts, weights, *refs):
    for (visit, tile), target in zip(wanted, refs[-len(wanted) :], strict=True):
        fill(target, weights.at[visit], ids, counts, visit, tile, item_count)


def visit_kernel(first, count, source, kept, joined, high, low, dense, items, *refs):
    new_items, errors, used = refs[-3:]
    start = 0
    for chunk in refs[len(refs) - 3 - joined : -3]:
        new_items[pl.ds(start, chunk.shape[0]), :] = chunk[...]
        start += chunk.shape[0]
    q, p = items[pl.ds(source, count), :], (high[...], low[...])
    e = errors_of(q, p, dense[pl.ds(first, count), :].astype(jnp.float32))
    new_items[pl.ds(start, count), :] = stepped(q, e, p)
    rows = pl.ds(kept, count)
    errors[rows, :] = e
    used[rows, :] = q


def early_kernel(split, errors, used, total):
    total[...] = gradient(errors[:split, :], used[:split, :])


def gradient_kernel(split, shares, errors, used, total, new_total, *parts):
    new_total[...] = total[...] + gradient(errors[split:, :], used[split:, :])
    share = total.shape[0] // shares
    for i, part in enumerate(parts):
        away, piece = i // PIECES + 1, i % PIECES
        size = part.shape[0]
        start = lax.rem(lax.axis_index("isec") + away, shares) * share + piece * size
        part[...] = new_total[pl.ds(pl.multiple_of(start, size), size), :]


def users_kernel(users, total, *refs):
    *received, new_users = refs
    share = new_users.shape[0]
    size = share // PIECES
    for piece in range(PIECES):
        start = lax.axis_index("isec") * share + piece * size
        rows = pl.ds(pl.multiple_of(start, size), size)
        summed = total[rows, :]
        for term in received[piece::PIECES]:
            summed = summed + term[...]
        p = users[rows, :]
        new_users[pl.ds(piece * size, size), :] = p - user_rate * (summed + shrinkage * p)


def place_kernel(*refs):
    *chunks, whole, moved = refs
    start, stores = 0, []
    for i, chunk in enumerate(chunks):
        target = whole.at[pl.ds(start, chunk.shape[0])]
        stores.append(pltpu.make_async_copy(chunk, target, moved.at[i]))
        start += chunk.shape[0]
    for store in stores:
        store.start()
    for store in stores:
        store.wait()


def call(kernel, name, out_shape, in_specs, args, flops=0, limit=LIMIT, **more):
    cost = pl.CostEstimate(flops=flops, bytes_accessed=MIB, transcendentals=0)
    return pl.pallas_call(
        kernel,
        name=name,
        out_shape=out_shape,
        in_specs=in_specs,
        cost_estimate=cost,
        compiler_params=pltpu.CompilerParams(vmem_limit_bytes=limit),
        **more,
    )(*args)


def on_device(user_factors, item_factors, confidence, tile_ids, tile_counts):
    visits = confidence.shape[2]
    user_rows, rank = user_factors.shape
    block_rows = item_factors.shape[0]
    item_count = block_rows // TILE
    sections = lax.axis_size("isec")
    weights, ids, counts = confidence[0, 0], tile_ids[0, 0], tile_counts[0, 0]
    unit = 2 * 3 * user_rows * rank

    def vmem(shape, dtype=jnp.float32):
        return pltpu.VMEM(shape, dtype)

    def in_hbm(*arrays):
        return tuple(pltpu.with_memory_space_constraint(array, pltpu.HBM) for array in arrays)

    sizes = (ROWS,) * (block_rows // ROWS)
    starts = [sum(sizes[:i]) for i in range(len(sizes))]
    kept_shape = (visits * block_rows, rank), (visits * block_rows, user_rows)
    chunk, errors, used, *ready, users, rest, lists = call(
        functools.partial(first_kernel, item_count),
        "first_visit",
        (
            vmem((sizes[0], rank)),
            vmem(kept_shape[1]),
            vmem(kept_shape[0]),
            vmem((user_rows, rank), jnp.bfloat16),
            vmem((user_rows, rank), jnp.bfloat16),
            vmem((user_rows, rank)),
            vmem((block_rows - sizes[0], rank)),
            vmem(weights.shape, weights.dtype),
        ),
        [HBM] * 5,
        in_hbm(ids, counts, user_factors, item_factors, weights),
        flops=2 * unit * sizes[0],
        out_specs=(VMEM,) * 8,
        scratch_shapes=[
            pltpu.VMEM((sizes[0], rank), jnp.float32),
            pltpu.VMEM(weights.shape[1:], weights.dtype),
            pltpu.VMEM((TILE, user_rows), jnp.float32),
            pltpu.SMEM(ids.shape, jnp.int32),
            pltpu.SMEM(counts.shape, jnp.int32),
            pltpu.SemaphoreType.DMA((7,)),
        ],
    )
    kept = (errors, used)

    def dense_call(wanted, after):
        return call(
            functools.partial(dense_kernel, wanted, item_count),
            "dense_tiles",
            (jax.ShapeDtypeStruct((TILE, user_rows), weights.dtype),) * len(wanted),
            [SMEM, SMEM] + [VMEM] * (1 + len(after)),
            (ids, counts, lists, *after),
            out_specs=(VMEM,) * len(wanted),
        )

    def visit_call(visit, c, dense, items, source, kept, after=(), joined=()):
        start, size = starts[c], sizes[c]
        return call(
            functools.partial(visit_kernel, start % TILE, size, source, visit * block_rows + start, len(joined)),
            "visit_update",
            (
                f32(size + sum(chunk.shape[0] for chunk in joined), rank),
                f32(*kept_shape[1]),
                f32(*kept_shape[0]),
            ),
            [VMEM] * (6 + len(after) + len(joined)),
            (*ready, dense, items, *kept, *after, *joined),
            flops=2 * unit * size,
            out_specs=(VMEM,) * 3,
            input_output_aliases={4: 1, 5: 2},
        )

    groups = (tuple(range(len(sizes) - 1)), (len(sizes) - 1,))
    chunks, returned = [chunk], []
    wanted = [(0, j) for j in range(item_count)] + [(1, 0)]
    dense = dict(zip(wanted, dense_call(wanted, ()), strict=True))
    for c in range(1, len(sizes)):
        chunk, *kept = visit_call(0, c, dense[0, starts[c] // TILE], rest, starts[c] - sizes[0], kept)
        chunks.append(chunk)
    split = visits // 2 * block_rows
    for visit in range(1, visits):
        for c in range(len(sizes)):
            tile = (visit, starts[c] // TILE)
            if tile not in dense:
                (dense[tile],) = dense_call([tile], kept)
            last = visit == visits - 1
            after = ()
            if last and c == min(EARLY, len(sizes) - 1):
                total = call(
                    functools.partial(early_kernel, split),
                    "early_gradient",
                    f32(user_rows, rank),
                    [VMEM] * 2,
                    kept,
                    flops=unit * split,
                    out_specs=VMEM,
                )
                after = (total,)
            group = next(group for group in groups if c in group)
            joined = [chunks[i] for i in group[:-1]] if last and c == group[-1] else ()
            chunks[c], *kept = visit_call(
                visit, c, dense[tile], shifted(chunks[c], "user", 1), 0, kept, after, joined
            )
            if last and c == group[-1]:
                returned.append(shifted(chunks[c], "user", 1 - visits))
    away = sections - 1
    total, *parts = call(
        functools.partial(gradient_kernel, split, sections),
        "user_gradient",
        (f32(user_rows, rank),) + (f32(user_rows // sections // PIECES, rank),) * (away * PIECES),
        [VMEM] * 3,
        (*kept, total),
        flops=unit * (visits * block_rows - split),
        out_specs=(VMEM,) * (1 + away * PIECES),
        input_output_aliases={2: 0},
    )

    received = [shifted(part, "isec", i // PIECES + 1) for i, part in enumerate(parts)]
    new_users = call(
        users_kernel,
        "new_users",
        f32(user_rows // sections, rank),
        [VMEM] * (2 + len(received)),
        (users, total, *received),
        limit=8 * MIB,
        out_specs=VMEM,
    )
    new_items = call(
        place_kernel,
        "place_items",
        f32(block_rows, rank),
        [VMEM] * len(returned),
        returned,
        limit=4 * MIB,
        out_specs=HBM,
        scratch_shapes=[pltpu.SemaphoreType.DMA((len(returned),))],
    )
    return new_users, new_items


def solution(mesh):
    return jax.shard_map(
        on_device,
        mesh=mesh,
        in_specs=(
            P("user", None),
            P(("user", "isec"), None),
            P("user", "isec", None, None, None, None),
            P("user", "isec", None, None),
            P("user", "isec", None),
        ),
        out_specs=(P(("user", "isec"), None), P(("user", "isec"), None)),
        check_vma=False,
    )
```

```python
import functools

import jax
import jax.numpy as jnp
from jax import lax
from jax.experimental import pallas as pl
from jax.experimental.pallas import tpu as pltpu
from jax.sharding import PartitionSpec as P

TILE = 128
ROWS = TILE // 2
PIECES = 4
EARLY = 1

item_rate = 0.02
user_rate = 0.005
shrinkage = 0.1

MIB = 1 << 20
LIMIT = 16 * MIB
SMEM, HBM, VMEM = (pl.BlockSpec(memory_space=s) for s in (pltpu.SMEM, pltpu.HBM, pltpu.VMEM))


def shifted(block, axis, distance):
    count = lax.axis_size(axis)
    return lax.ppermute(block, axis, [((i - distance) % count, i) for i in range(count)])


def f32(*shape):
    return jax.ShapeDtypeStruct(shape, jnp.float32)


def halves(x):
    high = x.astype(jnp.bfloat16)
    return high, (x - high.astype(jnp.float32)).astype(jnp.bfloat16)


def dot(a, b, left, right):
    dims = (((left,), (right,)), ((), ()))
    return lax.dot_general(a, b, dims, preferred_element_type=jnp.float32)


def product(a, b, right):
    count = a[0].shape[0]
    both = dot(jnp.concatenate(a, axis=0), b[0], 1, right)
    return both[:count] + (both[count:] + dot(a[0], b[1], 1, right))


def errors_of(q, p, weights):
    return weights * (product(halves(q), p, 1) - 1.0)


def stepped(q, error, p):
    return q - item_rate * (product(halves(error), p, 0) + shrinkage * q)


def gradient(error, q):
    e, r = halves(error), halves(q)
    both = dot(jnp.concatenate(e, axis=0), jnp.concatenate([r[0], r[0]], axis=0), 0, 0)
    return both + dot(e[0], r[1], 0, 0)


def fill(dense, lists, ids, counts, visit, first, item_count):
    dense[...] = jnp.zeros_like(dense)
    rows = dense.shape[0]
    for n in range(lists.shape[0]):
        k = ids[visit, n]
        row = (k % item_count - first) * TILE

        @pl.when((n < counts[visit]) & (row >= 0) & (row < rows))
        def _():
            place = (
                pl.ds(pl.multiple_of(row, TILE), TILE),
                pl.ds(pl.multiple_of(k // item_count * TILE, TILE), TILE),
            )
            dense[place] = lists[n].T.astype(dense.dtype)


def first_kernel(item_count, ids, counts, users, items, weights, *refs):
    new_items, errors, used, high, low, p_rows, rest, lists, *refs = refs
    q_rows, first_lists, dense, own_ids, own_counts, arrived = refs
    pairs = [
        (ids, own_ids),
        (counts, own_counts),
        (weights.at[0], first_lists),
        (items.at[pl.ds(0, q_rows.shape[0])], q_rows),
        (users, p_rows),
        (weights, lists),
    ]
    pairs.append((items.at[pl.ds(q_rows.shape[0], rest.shape[0])], rest))
    copies = [pltpu.make_async_copy(*pair, arrived.at[i]) for i, pair in enumerate(pairs)]
    for copy in copies:
        copy.start()
    for copy in copies[:3]:
        copy.wait()
    fill(dense, first_lists, own_ids, own_counts, 0, 0, item_count)
    copies[3].wait()
    q = q_rows[...]
    copies[4].wait()
    p = halves(p_rows[...])
    high[...], low[...] = p
    e = errors_of(q, p, dense[pl.ds(0, q.shape[0]), :])
    new_items[...] = stepped(q, e, p)
    errors[pl.ds(0, q.shape[0]), :] = e
    used[pl.ds(0, q.shape[0]), :] = q
    for copy in copies[5:]:
        copy.wait()


def dense_kernel(wanted, item_count, ids, counts, weights, *refs):
    for (visit, tile), target in zip(wanted, refs[-len(wanted) :], strict=True):
        fill(target, weights.at[visit], ids, counts, visit, tile, item_count)


def visit_kernel(first, count, source, kept, joined, high, low, dense, items, *refs):
    new_items, errors, used = refs[-3:]
    start = 0
    for chunk in refs[len(refs) - 3 - joined : -3]:
        new_items[pl.ds(start, chunk.shape[0]), :] = chunk[...]
        start += chunk.shape[0]
    q, p = items[pl.ds(source, count), :], (high[...], low[...])
    e = errors_of(q, p, dense[pl.ds(first, count), :].astype(jnp.float32))
    new_items[pl.ds(start, count), :] = stepped(q, e, p)
    rows = pl.ds(kept, count)
    errors[rows, :] = e
    used[rows, :] = q


def early_kernel(split, errors, used, total):
    total[...] = gradient(errors[:split, :], used[:split, :])


def gradient_kernel(split, shares, errors, used, total, new_total, *parts):
    new_total[...] = total[...] + gradient(errors[split:, :], used[split:, :])
    share = total.shape[0] // shares
    for i, part in enumerate(parts):
        away, piece = i // PIECES + 1, i % PIECES
        size = part.shape[0]
        start = lax.rem(lax.axis_index("isec") + away, shares) * share + piece * size
        part[...] = new_total[pl.ds(pl.multiple_of(start, size), size), :]


def users_kernel(users, total, *refs):
    *received, new_users = refs
    share = new_users.shape[0]
    size = share // PIECES
    for piece in range(PIECES):
        start = lax.axis_index("isec") * share + piece * size
        rows = pl.ds(pl.multiple_of(start, size), size)
        summed = total[rows, :]
        for term in received[piece::PIECES]:
            summed = summed + term[...]
        p = users[rows, :]
        new_users[pl.ds(piece * size, size), :] = p - user_rate * (summed + shrinkage * p)


def place_kernel(first, chunk, *refs):
    whole, moved = refs[-2:]
    store = pltpu.make_async_copy(chunk, whole.at[pl.ds(first, chunk.shape[0])], moved)
    store.start()
    store.wait()


def call(kernel, name, out_shape, in_specs, args, flops=0, limit=LIMIT, **more):
    cost = pl.CostEstimate(flops=flops, bytes_accessed=MIB, transcendentals=0)
    return pl.pallas_call(
        kernel,
        name=name,
        out_shape=out_shape,
        in_specs=in_specs,
        cost_estimate=cost,
        compiler_params=pltpu.CompilerParams(vmem_limit_bytes=limit),
        **more,
    )(*args)


def on_device(user_factors, item_factors, confidence, tile_ids, tile_counts):
    visits = confidence.shape[2]
    user_rows, rank = user_factors.shape
    block_rows = item_factors.shape[0]
    item_count = block_rows // TILE
    sections = lax.axis_size("isec")
    weights, ids, counts = confidence[0, 0], tile_ids[0, 0], tile_counts[0, 0]
    unit = 2 * 3 * user_rows * rank

    def vmem(shape, dtype=jnp.float32):
        return pltpu.VMEM(shape, dtype)

    def in_hbm(*arrays):
        return tuple(pltpu.with_memory_space_constraint(array, pltpu.HBM) for array in arrays)

    sizes = (ROWS,) * (block_rows // ROWS)
    starts = [sum(sizes[:i]) for i in range(len(sizes))]
    kept_shape = (visits * block_rows, rank), (visits * block_rows, user_rows)
    chunk, errors, used, *ready, users, rest, lists = call(
        functools.partial(first_kernel, item_count),
        "first_visit",
        (
            vmem((sizes[0], rank)),
            vmem(kept_shape[1]),
            vmem(kept_shape[0]),
            vmem((user_rows, rank), jnp.bfloat16),
            vmem((user_rows, rank), jnp.bfloat16),
            vmem((user_rows, rank)),
            vmem((block_rows - sizes[0], rank)),
            vmem(weights.shape, weights.dtype),
        ),
        [HBM] * 5,
        in_hbm(ids, counts, user_factors, item_factors, weights),
        flops=2 * unit * sizes[0],
        out_specs=(VMEM,) * 8,
        scratch_shapes=[
            pltpu.VMEM((sizes[0], rank), jnp.float32),
            pltpu.VMEM(weights.shape[1:], weights.dtype),
            pltpu.VMEM((TILE, user_rows), jnp.float32),
            pltpu.SMEM(ids.shape, jnp.int32),
            pltpu.SMEM(counts.shape, jnp.int32),
            pltpu.SemaphoreType.DMA((7,)),
        ],
    )
    kept = (errors, used)

    def dense_call(wanted, after):
        return call(
            functools.partial(dense_kernel, wanted, item_count),
            "dense_tiles",
            (jax.ShapeDtypeStruct((TILE, user_rows), weights.dtype),) * len(wanted),
            [SMEM, SMEM] + [VMEM] * (1 + len(after)),
            (ids, counts, lists, *after),
            out_specs=(VMEM,) * len(wanted),
        )

    def visit_call(visit, c, dense, items, source, kept, after=(), joined=()):
        start, size = starts[c], sizes[c]
        return call(
            functools.partial(visit_kernel, start % TILE, size, source, visit * block_rows + start, len(joined)),
            "visit_update",
            (
                f32(size + sum(chunk.shape[0] for chunk in joined), rank),
                f32(*kept_shape[1]),
                f32(*kept_shape[0]),
            ),
            [VMEM] * (6 + len(after) + len(joined)),
            (*ready, dense, items, *kept, *after, *joined),
            flops=2 * unit * size,
            out_specs=(VMEM,) * 3,
            input_output_aliases={4: 1, 5: 2},
        )

    groups = (tuple(range(len(sizes) - 1)), (len(sizes) - 1,))
    chunks, returned = [chunk], []
    wanted = [(0, j) for j in range(item_count)] + [(1, 0)]
    dense = dict(zip(wanted, dense_call(wanted, ()), strict=True))
    for c in range(1, len(sizes)):
        chunk, *kept = visit_call(0, c, dense[0, starts[c] // TILE], rest, starts[c] - sizes[0], kept)
        chunks.append(chunk)
    split = visits // 2 * block_rows
    for visit in range(1, visits):
        for c in range(len(sizes)):
            tile = (visit, starts[c] // TILE)
            if tile not in dense:
                (dense[tile],) = dense_call([tile], kept)
            last = visit == visits - 1
            after = ()
            if last and c == min(EARLY, len(sizes) - 1):
                total = call(
                    functools.partial(early_kernel, split),
                    "early_gradient",
                    f32(user_rows, rank),
                    [VMEM] * 2,
                    kept,
                    flops=unit * split,
                    out_specs=VMEM,
                )
                after = (total,)
            group = next(group for group in groups if c in group)
            joined = [chunks[i] for i in group[:-1]] if last and c == group[-1] else ()
            chunks[c], *kept = visit_call(
                visit, c, dense[tile], shifted(chunks[c], "user", 1), 0, kept, after, joined
            )
            if last and c == group[-1]:
                returned.append(shifted(chunks[c], "user", 1 - visits))
    away = sections - 1
    total, *parts = call(
        functools.partial(gradient_kernel, split, sections),
        "user_gradient",
        (f32(user_rows, rank),) + (f32(user_rows // sections // PIECES, rank),) * (away * PIECES),
        [VMEM] * 3,
        (*kept, total),
        flops=unit * (visits * block_rows - split),
        out_specs=(VMEM,) * (1 + away * PIECES),
        input_output_aliases={2: 0},
    )

    received = [shifted(part, "isec", i // PIECES + 1) for i, part in enumerate(parts)]
    new_users = call(
        users_kernel,
        "new_users",
        f32(user_rows // sections, rank),
        [VMEM] * (2 + len(received)),
        (users, total, *received),
        limit=8 * MIB,
        out_specs=VMEM,
    )
    new_items = ()
    for group, rows in zip(groups, returned, strict=True):
        new_items = (
            call(
                functools.partial(place_kernel, starts[group[0]]),
                "place_items",
                f32(block_rows, rank),
                [VMEM] + [HBM] * len(new_items),
                (rows, *new_items),
                limit=4 * MIB,
                out_specs=HBM,
                scratch_shapes=[pltpu.SemaphoreType.DMA],
                input_output_aliases={1: 0} if new_items else {},
            ),
        )
    (new_items,) = new_items
    return new_users, new_items


def solution(mesh):
    return jax.shard_map(
        on_device,
        mesh=mesh,
        in_specs=(
            P("user", None),
            P(("user", "isec"), None),
            P("user", "isec", None, None, None, None),
            P("user", "isec", None, None),
            P("user", "isec", None),
        ),
        out_specs=(P(("user", "isec"), None), P(("user", "isec"), None)),
        check_vma=False,
    )
```
